32 devices in a mesh: req: 4 (over y, core), exp: 8 (over z, x).
Axes of the slice: x: 2, y: 2, z: 4, core: 2. Of those that a mesh axis runs over, the one named last changes fastest.
Arguments:
- hidden_in: bfloat16 [4096, 2048], P(('req', 'exp')), may hold values from -6 to 6
- qkv: bfloat16 [4096, 6144], P(('req', 'exp'))
- q_gain: float32 [128], replicated, as said below
- k_gain: float32 [128], replicated, as said below
- query_pages: bfloat16 [4, 8, 128, 4096], P('req', None, None, 'exp'), may hold values from -6 to 6
- page_table: int32 [4, 8], P('req'), may hold values from 0 to 7, each once within a row
- doc_lengths: int32 [4, 32], P('req'), may hold values from 1 to 128, 1024 in all within a row
- doc_query: int32 [4, 32], P('req'), may hold values from 0 to 7
- out_weight: bfloat16 [2048, 2048], replicated, may hold values from -0.125 to 0.125
- moe_gain: float32 [2048], replicated, may hold values from 0.5 to 1.5
- routes: int32 [4096, 8], P(('req', 'exp')), may hold values from 0 to 15, all different within a row; in each aligned block of 128 rows (0 to 127, 128 to 255, ...) at most 96 rows name the same one
- route_weight: float32 [4096, 8], P(('req', 'exp')), may hold values from 0.02 to 0.25
- gate_weight: bfloat16 [32, 2048, 512], P(('req', 'exp')), may hold values from -0.125 to 0.125
- up_weight: bfloat16 [32, 2048, 512], P(('req', 'exp')), may hold values from -0.125 to 0.125
- down_weight: bfloat16 [32, 512, 2048], P(('req', 'exp')), may hold values from -0.1875 to 0.1875
- score_weight: float32 [2048], replicated, may hold values from -0.125 to 0.125
Outputs:
- layer_out: bfloat16 [4096, 2048], P(('req', 'exp'))
- doc_scores: float32 [4, 32], P('req')
The draws below stay inside these ranges and needn't reach their ends.
Inputs may be any that keep to these rules, and one draw needn't show every extreme that they name: Among the routes of the rows of one device no expert is named more than 96 times; in every draw some device's rows name some expert exactly 96 times. `doc_lengths`: each group's 32 lengths sum to 1024; the longest of each group is exactly 128. `page_table`: each row is a permutation of the pages. `q_gain`: Positive. `k_gain`: Positive.
All inputs are finite; a program needn't handle non-finite values.
Results may differ from the reference program's by a relative error of at most 0.012.
Values may be sent and summed in bfloat16 or wider, within the bound.
No kernel may reach another device: no remote copies, remote signals or barrier semaphores. Data moves between devices by JAX's collectives and lax.ppermute only.
A program may use at most 128 MiB of HBM per device.

```python
import math
import jax
import jax.numpy as jnp
import numpy as np
from jax import lax

D = 2048
HEADS = 16
HD = 128
FF = 1024
TOP = 8
TOK_DEV = 128
DOCS = 32
NQ = 8
PAGE = 128
HALF = 512
EXPERTS = 16
GROUP = 1024
TOKENS = 4096
CAP = 96
N_REQ = 4
N_EXP = 8


def draw_qkv(key, part):
    values = jax.random.normal(key, (TOKENS, 3 * D), jnp.float32)
    return values.astype(jnp.bfloat16)


def draw_q_gain(key, part):
    return jax.random.uniform(jax.random.fold_in(key, 11), (HD,), jnp.float32, 0.6, 1.6)


def draw_k_gain(key, part):
    return jax.random.uniform(jax.random.fold_in(key, 23), (HD,), jnp.float32, 0.6, 1.6)


def touch_ends(array, stream_key, low, largest):
    spot = [jax.random.randint(jax.random.fold_in(stream_key, axis), (), 0, length) for axis, length in enumerate(array.shape)]
    widest = array.shape.index(max(array.shape))
    next_to = spot[:widest] + [(spot[widest] + 1) % array.shape[widest]] + spot[widest + 1:]
    return array.at[tuple(spot)].set(low).at[tuple(next_to)].set(largest)


def block_scale(own_key, dims, split, smallest, top_value):
    def one(position, blocks):
        steps = jax.random.uniform(jax.random.fold_in(jax.random.fold_in(own_key, 6), position), (blocks,), jnp.float32, smallest / len(split), top_value / len(split))
        return jnp.repeat(jnp.exp(steps), dims[position] // blocks).reshape((-1,) + (1,) * (len(dims) - position - 1))

    gain = one(*split[0])
    for cut in split[1:]:
        gain = gain * one(*cut)
    return gain


def profile(count, total, most, lean):
    loads = [(1 << 20) // math.isqrt(rank ** lean) + 1 for rank in range(2, count + 1)]
    spare, counts = total - most - (count - 1), [1] * (count - 1)
    while spare > 0:
        free = [i for i in range(count - 1) if counts[i] < most]
        mass, remaining = sum([loads[i] for i in free]), spare
        for i in free:
            extra = min(most - counts[i], max(1, remaining * loads[i] // mass), spare)
            counts[i] = counts[i] + extra
            spare = spare - extra
    return np.array([most] + counts)


def uneven(rng, amount, total, most, skew):
    if amount == 2:
        one = jax.random.randint(rng, (), max(1, total - most), min(most, total - 1) + 1)
        return jnp.stack([one, total - one])
    sizes = jnp.asarray(profile(amount, total, most, skew), jnp.int32)
    pairs = (amount - 1) // 2
    donor, receiver = sizes[1:1 + 2 * pairs:2], sizes[2:2 + 2 * pairs:2]
    slack = jnp.minimum(donor - 1, most - receiver)
    shifted = jax.random.randint(jax.random.fold_in(rng, 1), (pairs,), 0, 1 << 20) % (slack + 1)
    sizes = sizes.at[1:1 + 2 * pairs:2].set(donor - shifted).at[2:2 + 2 * pairs:2].set(receiver + shifted)
    return sizes[jax.random.permutation(jax.random.fold_in(rng, 2), amount)]


def shared_out(key, own, number, rows, amount, top, reach, lean):
    order = jax.random.permutation(key, amount)
    crowded, ordinary = shares(amount, rows * top, reach, lean, True), shares(amount, rows * top, reach, lean, False)
    places = jnp.arange(amount)

    def named(lengths, turn):
        used = int((lengths > 0).sum())
        fixed = max(1, used // 4)
        passed = fixed + (places - fixed + turn * (used - fixed)) % max(1, amount - fixed)
        return jnp.zeros((amount,), jnp.int32).at[order[jnp.where(places < fixed, places, passed)]].set(jnp.asarray(lengths, jnp.int32))

    lengths = jnp.where(number % 4 == 0, named(crowded, number // 4), named(ordinary, number - number // 4 - 1))
    mixed = jax.random.permutation(jax.random.fold_in(own, 3), amount)
    source_of, sink = mixed[0:amount // 2 * 2:2], mixed[1:amount // 2 * 2:2]
    margin = jnp.minimum(lengths[source_of] - 1, reach - lengths[sink]) // 2
    margin = jnp.where((source_of == order[0]) | (sink == order[0]) | (lengths[sink] == 0), 0, jnp.maximum(margin, 0))
    passed = jax.random.randint(jax.random.fold_in(own, 4), (amount // 2,), 0, 1 << 20) % (margin + 1)
    lengths = lengths.at[source_of].add(-passed).at[sink].add(passed)
    items = jnp.searchsorted(jnp.cumsum(lengths), jnp.arange(rows * top), side="right").astype(jnp.int32)
    table = items.reshape(top, rows).T
    table = table[jax.random.permutation(jax.random.fold_in(own, 1), rows)]
    turn = jax.random.randint(jax.random.fold_in(own, 2), (rows, 1), 0, top)
    return jnp.take_along_axis(table, (jnp.arange(top)[None, :] + turn) % top, axis=1)


def shares(number_of, total, reach, skew, full):
    weights = [(1 << 20) // math.isqrt(standing ** skew) + 1 for standing in range(1, number_of + 1)]
    largest = reach if full else min(reach, max(-(-total // number_of), total * weights[0] // sum(weights)))
    least = 1 if total - largest >= number_of - 1 else 0
    counts, surplus = [largest] + [least] * (number_of - 1), total - largest - least * (number_of - 1)
    while surplus > 0:
        movable = [i for i in range(1, number_of) if counts[i] < largest] or [i for i in range(1, number_of) if counts[i] < reach]
        whole, remaining = sum([weights[i] for i in movable]), surplus
        for i in movable:
            more = min(reach - counts[i], max(1, remaining * weights[i] // whole), surplus)
            counts[i] = counts[i] + more
            surplus = surplus - more
    return np.array(counts)


def bell_draw(key, dims, deviation, most, cuts=(), kind=jnp.bfloat16):
    factor_of = block_scale(key, dims, cuts, -0.22, 0.18) if cuts else 1.0
    values = jax.random.normal(key, dims, jnp.float32) * deviation * factor_of
    return jnp.minimum(jnp.maximum(values, -most), most).astype(kind)


def setup_inputs(seed: int = 0) -> dict:
    key_list = jax.random.split(jax.random.key(seed), 17)
    hidden_in = bell_draw(key_list[0], (TOKENS, D), 1.0, 6.0, ((0, 32),))
    qkv = draw_qkv(jax.random.fold_in(key_list[16], 71), 0)
    q_gain = draw_q_gain(jax.random.fold_in(key_list[16], 71), 0)
    k_gain = draw_k_gain(jax.random.fold_in(key_list[16], 71), 0)
    query_pages = bell_draw(key_list[4], (N_REQ, NQ, PAGE, 2 * D), 1.0, 6.0, ((0, 4), (3, 8)))
    page_table = jax.vmap(lambda own: jax.random.permutation(own, NQ))(jax.random.split(key_list[5], N_REQ)).reshape((N_REQ, NQ)).astype(jnp.int32)
    doc_lengths = jax.vmap(lambda own: uneven(own, DOCS, GROUP, TOK_DEV, 2))(jax.random.split(key_list[6], N_REQ)).reshape((N_REQ, DOCS)).astype(jnp.int32)
    doc_query = touch_ends(jax.random.randint(key_list[7], (N_REQ, DOCS), 0, NQ), jax.random.fold_in(key_list[7], 1), 0, NQ - 1).astype(jnp.int32)
    out_weight = bell_draw(key_list[8], (D, D), D ** -0.5, 0.125)
    moe_gain = jnp.clip(1.0 + 0.1 * jax.random.normal(key_list[9], (D,), jnp.float32), 0.5, 1.5)
    routes_keys = jax.random.split(jax.random.fold_in(key_list[10], 1), TOKENS // TOK_DEV)
    routes_turns = jax.random.permutation(jax.random.fold_in(key_list[10], 3), TOKENS // TOK_DEV)
    routes = jax.vmap(lambda own, number: shared_out(jax.random.fold_in(key_list[10], 2), own, number, TOK_DEV, EXPERTS, TOP, CAP, 2))(routes_keys, routes_turns).reshape((TOKENS, TOP))
    route_weight = jnp.clip(0.02 + 0.23 * jax.random.uniform(key_list[11], (TOKENS, TOP), jnp.float32) ** block_scale(key_list[11], (TOKENS, TOP), ((0, 32),), -0.2, 0.2), 0.02, 0.25)
    gate_weight = bell_draw(key_list[12], (2 * EXPERTS, D, HALF), D ** -0.5, 0.125, ((0, 32),))
    up_weight = bell_draw(key_list[13], (2 * EXPERTS, D, HALF), D ** -0.5, 0.125, ((0, 32),))
    down_weight = bell_draw(key_list[14], (2 * EXPERTS, HALF, D), FF ** -0.5, 0.1875, ((0, 32),))
    score_weight = bell_draw(key_list[15], (D,), D ** -0.5, 0.125, (), jnp.float32)
    return {"hidden_in": hidden_in, "qkv": qkv, "q_gain": q_gain, "k_gain": k_gain, "query_pages": query_pages, "page_table": page_table, "doc_lengths": doc_lengths, "doc_query": doc_query, "out_weight": out_weight, "moe_gain": moe_gain, "routes": routes, "route_weight": route_weight, "gate_weight": gate_weight, "up_weight": up_weight, "down_weight": down_weight, "score_weight": score_weight}


eps = 1e-06
rope_base = 50000.0
neg_fill = -1e+30

def rms_scale(values, gain_vec):
    mean_sq = lax.optimization_barrier(jnp.mean(values * values, axis=-1, keepdims=True))
    return values * lax.rsqrt(mean_sq + eps) * gain_vec

def rotate(values, positions):
    half_dim = values.shape[-1] // 2
    frequency = rope_base ** (-(jnp.arange(half_dim, dtype=jnp.float32) * 2.0 / values.shape[-1]))
    angles = positions.astype(jnp.float32)[:, None] * frequency[None, :]
    cosine = jnp.cos(angles)[:, None, :]
    sine_part = jnp.sin(angles)[:, None, :]
    lower_part = values[..., :half_dim]
    upper_part = values[..., half_dim:]
    return jnp.concatenate([lower_part * cosine - upper_part * sine_part, upper_part * cosine + lower_part * sine_part], axis=-1)

def doc_table(doc_len, positions):
    doc_ends = jnp.cumsum(doc_len, dtype=jnp.int32)
    starts = doc_ends - doc_len
    doc_ids = lax.optimization_barrier(jnp.sum((positions[:, None] >= doc_ends[None, :]).astype(jnp.int32), axis=1, dtype=jnp.int32))
    inside = (positions >= 0) & (positions < doc_ends[-1])
    doc_ids = jnp.where(inside, doc_ids, -1)
    member = doc_ids[:, None] == jnp.arange(doc_len.shape[0], dtype=jnp.int32)[None, :]
    doc_start = lax.optimization_barrier(jnp.sum(jnp.where(member, starts[None, :], 0), axis=1, dtype=jnp.int32))
    return (doc_ids, member, doc_start)

def attend(query_rows, key_rows, value_rows, visible):
    score_scale = query_rows.shape[-1] ** (-0.5)
    scores = jnp.einsum('nhd,khd->hnk', query_rows.astype(jnp.float32), key_rows.astype(jnp.float32), precision=lax.Precision.HIGHEST) * score_scale
    scores = jnp.where(visible[None], scores, neg_fill)
    row_max = lax.optimization_barrier(jnp.max(scores, axis=-1))
    probs = jnp.where(visible[None], jnp.exp(scores - row_max[..., None]), 0.0)
    row_total = lax.optimization_barrier(jnp.sum(probs, axis=-1))
    rounded = lax.optimization_barrier(probs.astype(jnp.bfloat16)).astype(jnp.float32)
    weighted = jnp.einsum('hnk,khd->nhd', rounded, value_rows.astype(jnp.float32), precision=lax.Precision.HIGHEST)
    return (weighted, row_max.T, row_total.T)

def slot_numbers(route_flat, bin_count):
    onehot = (route_flat[:, None] == jnp.arange(bin_count, dtype=jnp.int32)[None, :]).astype(jnp.int32)
    prior_count = jnp.cumsum(onehot, axis=0, dtype=jnp.int32) - onehot
    return lax.optimization_barrier(jnp.sum(prior_count * onehot, axis=1, dtype=jnp.int32))

def reference(hidden_in, qkv, q_gain, k_gain, query_pages, page_table, doc_lengths, doc_query, out_weight, moe_gain, routes, route_weight, gate_weight, up_weight, down_weight, score_weight):
    devices = N_REQ * N_EXP
    group_len = TOK_DEV * N_EXP
    positions = jnp.arange(group_len, dtype=jnp.int32)
    doc_ids, member, doc_start = jax.vmap(lambda doc_len: doc_table(doc_len, positions))(doc_lengths)
    rope_pos = (PAGE + positions[None, :] - doc_start).reshape(-1)
    query_rows = rotate(rms_scale(qkv[:, :D].astype(jnp.float32).reshape(TOKENS, HEADS, HD), q_gain), rope_pos).astype(jnp.bfloat16)
    key_rows = rotate(rms_scale(qkv[:, D:2 * D].astype(jnp.float32).reshape(TOKENS, HEADS, HD), k_gain), rope_pos).astype(jnp.bfloat16)
    value_rows = qkv[:, 2 * D:].reshape(TOKENS, HEADS, HD)
    pad_spec = ((0, 0), (TOK_DEV, TOK_DEV), (0, 0), (0, 0))
    key_pad = jnp.pad(key_rows.reshape(N_REQ, group_len, HEADS, HD), pad_spec)
    value_pad = jnp.pad(value_rows.reshape(N_REQ, group_len, HEADS, HD), pad_spec)
    doc_pad = jnp.pad(doc_ids, ((0, 0), (TOK_DEV, TOK_DEV)), constant_values=-1)
    query_ids = jnp.take_along_axis(doc_query, doc_ids, axis=1)
    page_of_tok = jnp.take_along_axis(page_table, query_ids, axis=1)
    pool = query_pages.reshape(N_REQ, NQ * PAGE, HEADS, 2, HD)
    key_page = jnp.arange(NQ * PAGE, dtype=jnp.int32) // PAGE

    def block_attn(block):
        group_id = block // N_EXP
        column_id = block % N_EXP
        own_query = lax.dynamic_slice_in_dim(query_rows, block * TOK_DEV, TOK_DEV, 0)
        own_keys = lax.dynamic_slice_in_dim(lax.dynamic_index_in_dim(key_pad, group_id, 0, False), column_id * TOK_DEV, 3 * TOK_DEV, 0)
        own_values = lax.dynamic_slice_in_dim(lax.dynamic_index_in_dim(value_pad, group_id, 0, False), column_id * TOK_DEV, 3 * TOK_DEV, 0)
        own_doc = lax.dynamic_slice_in_dim(lax.dynamic_index_in_dim(doc_ids, group_id, 0, False), column_id * TOK_DEV, TOK_DEV, 0)
        win_doc = lax.dynamic_slice_in_dim(lax.dynamic_index_in_dim(doc_pad, group_id, 0, False), column_id * TOK_DEV, 3 * TOK_DEV, 0)
        own_page = lax.dynamic_slice_in_dim(lax.dynamic_index_in_dim(page_of_tok, group_id, 0, False), column_id * TOK_DEV, TOK_DEV, 0)
        group_pool = lax.dynamic_index_in_dim(pool, group_id, 0, False)
        all_keys = jnp.concatenate([group_pool[:, :, 0], own_keys], axis=0)
        all_values = jnp.concatenate([group_pool[:, :, 1], own_values], axis=0)
        visible = jnp.concatenate([key_page[None, :] == own_page[:, None], win_doc[None, :] == own_doc[:, None]], axis=1)
        weighted, row_max, row_total = attend(own_query, all_keys, all_values, visible)
        return (weighted / row_total[..., None]).astype(jnp.bfloat16).reshape(TOK_DEV, D)
    attn = lax.map(block_attn, jnp.arange(devices, dtype=jnp.int32)).reshape(TOKENS, D)
    mixed = jnp.dot(attn, out_weight, preferred_element_type=jnp.float32)
    resid = (hidden_in.astype(jnp.float32) + mixed).astype(jnp.bfloat16)
    normed = rms_scale(resid.astype(jnp.float32), moe_gain).astype(jnp.bfloat16)
    route_blocks = routes.reshape(devices, TOK_DEV * TOP)
    weight_blocks = route_weight.reshape(devices, TOK_DEV * TOP)
    slots = jax.vmap(lambda route_flat: slot_numbers(route_flat, EXPERTS))(route_blocks)
    place = route_blocks * CAP + slots
    token_ids = jnp.broadcast_to((jnp.arange(TOK_DEV * TOP, dtype=jnp.int32) // TOP)[None, :], (devices, TOK_DEV * TOP))
    table = jax.vmap(lambda spots, tokens_of: jnp.full((EXPERTS * CAP,), TOK_DEV, jnp.int32).at[spots].set(tokens_of))(place, token_ids)
    weight_table = jax.vmap(lambda spots, route_w: jnp.zeros((EXPERTS * CAP,), jnp.float32).at[spots].set(route_w))(place, weight_blocks)
    normed_blocks = jnp.concatenate([normed.reshape(devices, TOK_DEV, D), jnp.zeros((devices, 1, D), jnp.bfloat16)], axis=1)
    block_rows = jnp.arange(devices, dtype=jnp.int32)[:, None]

    def expert_step(running, expert_id):
        slot_tokens = lax.dynamic_slice_in_dim(table, expert_id * CAP, CAP, 1)
        slot_weights = lax.dynamic_slice_in_dim(weight_table, expert_id * CAP, CAP, 1)
        token_rows = normed_blocks[block_rows, slot_tokens].reshape(devices * CAP, D)
        summed = jnp.zeros((devices * CAP, D), jnp.float32)
        for side_index in range(2):
            piece_id = 2 * expert_id + side_index
            gate_act = jnp.dot(token_rows, lax.dynamic_index_in_dim(gate_weight, piece_id, 0, False), preferred_element_type=jnp.float32)
            up_act = jnp.dot(token_rows, lax.dynamic_index_in_dim(up_weight, piece_id, 0, False), preferred_element_type=jnp.float32)
            hidden_act = (jax.nn.silu(gate_act) * up_act).astype(jnp.bfloat16)
            piece_out = jnp.dot(hidden_act, lax.dynamic_index_in_dim(down_weight, piece_id, 0, False), preferred_element_type=jnp.float32)
            summed = summed + lax.optimization_barrier(piece_out.astype(jnp.bfloat16)).astype(jnp.float32)
        result = lax.optimization_barrier(summed.astype(jnp.bfloat16)).astype(jnp.float32).reshape(devices, CAP, D)
        running = running.at[block_rows, slot_tokens].add(result * slot_weights[..., None])
        return (running, None)
    combined, unused = lax.scan(expert_step, jnp.zeros((devices, TOK_DEV + 1, D), jnp.float32), jnp.arange(EXPERTS, dtype=jnp.int32))
    layer_out = (resid.astype(jnp.float32) + combined[:, :TOK_DEV].reshape(TOKENS, D)).astype(jnp.bfloat16)
    token_score = jnp.dot(layer_out.astype(jnp.float32), score_weight, precision=lax.Precision.HIGHEST).reshape(N_REQ, group_len)
    doc_sums = jnp.einsum('rg,rgd->rd', token_score, member.astype(jnp.float32), precision=lax.Precision.HIGHEST)
    doc_scores = doc_sums / doc_lengths.astype(jnp.float32)
    return (layer_out, doc_scores)
```

```python
import functools

import jax
import jax.numpy as jnp
import numpy as np
from jax import lax
from jax.experimental import pallas as pl
from jax.experimental.pallas import tpu as pltpu
from jax.sharding import PartitionSpec as P

HEADS = 16
HD = 128
TOP = 8
PAGE = 128
LANES = 128
ALL = ("req", "exp")


eps = 1e-06
rope_base = 50000.0
neg_fill = -1e30


def rms_scale(values, gain_vec):
    mean_sq = jnp.mean(values * values, axis=-1, keepdims=True)
    return values * lax.rsqrt(mean_sq + eps) * gain_vec


def rope_table():
    half_dim = HD // 2
    frequency = rope_base ** (-(np.arange(half_dim) * 2.0 / HD))
    angles = (PAGE + np.arange(PAGE))[:, None] * frequency[None, :]
    cosine, sine = np.cos(angles), np.sin(angles)
    rest = np.concatenate([cosine, cosine, -sine, sine], axis=1).astype(np.float32)
    terms = []
    for _ in range(3):
        term = rest.astype(jnp.bfloat16)
        terms.append(term)
        rest = rest - term.astype(np.float32)
    return np.concatenate(terms, axis=1)


def attention_kernel(
    qkv_ref, pages_ref, len_ref, query_ref, table_ref, q_gain_ref, k_gain_ref, rope_ref,
    out_ref, q_rows, k_rows,
):
    tokens = qkv_ref.shape[0]
    heads = qkv_ref.shape[1] // (3 * HD)
    blocks = tokens // LANES
    keys = pages_ref.shape[0]
    score_scale = HD ** (-0.5) * 1.4426950408889634

    row_ids = lax.broadcasted_iota(jnp.int32, (LANES, LANES), 0)
    lane_ids = lax.broadcasted_iota(jnp.int32, (LANES, LANES), 1)
    lane_f32 = lane_ids.astype(jnp.float32)
    upper = (row_ids <= lane_ids).astype(jnp.bfloat16)
    lens = jnp.broadcast_to(len_ref[...].astype(jnp.bfloat16), (16, LANES))
    ends = jnp.dot(lens, upper, preferred_element_type=jnp.float32)[0:1]
    slot = lax.broadcasted_iota(jnp.int32, (table_ref.shape[0], LANES), 0)
    doc_page = jnp.sum(
        jnp.where(slot == query_ref[...], table_ref[...], 0).astype(jnp.float32),
        axis=0, keepdims=True,
    )

    def places(block):
        own = (row_ids + block * LANES).astype(jnp.float32)
        passed = own >= ends
        start = jnp.max(jnp.where(passed, ends, 0.0), axis=1, keepdims=True)
        stop = jnp.min(jnp.where(passed, 1e9, ends), axis=1, keepdims=True)
        doc = jnp.sum(passed.astype(jnp.float32), axis=1, keepdims=True)
        page = jnp.sum(jnp.where(lane_f32 == doc, doc_page, 0.0), axis=1, keepdims=True)
        return own, start, stop, page

    @pl.loop(0, blocks)
    def _(block):
        rows = pl.ds(pl.multiple_of(block * LANES, LANES), LANES)
        own, start, _, _ = places(block)
        onehot = (lane_f32 == own - start).astype(jnp.bfloat16)
        terms = jnp.dot(onehot, rope_ref[...], preferred_element_type=jnp.float32)
        both = terms[:, : 2 * HD] + (terms[:, 2 * HD : 4 * HD] + terms[:, 4 * HD :])
        cosine, sine = both[:, :HD], both[:, HD:]
        for part, gain_ref, kept in ((0, q_gain_ref, q_rows), (1, k_gain_ref, k_rows)):
            for head in range(heads):
                at = (part * heads + head) * HD
                values = qkv_ref[rows, at : at + HD].astype(jnp.float32)
                values = rms_scale(values, gain_ref[...])
                swapped = pltpu.roll(values, HD // 2, 1)
                kept[rows, head * HD : (head + 1) * HD] = (
                    values * cosine + swapped * sine
                ).astype(jnp.bfloat16)

    page_of_key = (
        lax.broadcasted_iota(jnp.int32, (LANES, keys), 1) // PAGE
    ).astype(jnp.float32)
    wide = 3 * LANES
    key_at = lax.broadcasted_iota(jnp.int32, (LANES, wide), 1)

    @pl.loop(0, blocks)
    def _(block):
        rows = pl.ds(pl.multiple_of(block * LANES, LANES), LANES)
        first = pl.multiple_of(jnp.clip(block - 1, 0, blocks - 3) * LANES, LANES)
        window = pl.ds(first, wide)
        _, start, stop, page = places(block)
        position = (key_at + first).astype(jnp.float32)
        in_page = page_of_key == page
        in_doc = (position >= start) & (position < stop)
        for head in range(heads):
            cols = slice(head * HD, (head + 1) * HD)
            query = q_rows[rows, cols]
            page_keys = pages_ref[:, 2 * head * HD : (2 * head + 1) * HD]
            page_values = pages_ref[:, (2 * head + 1) * HD : (2 * head + 2) * HD]
            at = (2 * heads + head) * HD
            contract = (((1,), (1,)), ((), ()))
            far = lax.dot_general(
                query, page_keys, contract, preferred_element_type=jnp.float32
            )
            near = lax.dot_general(
                query, k_rows[window, cols], contract, preferred_element_type=jnp.float32
            )
            far = jnp.where(in_page, far, neg_fill)
            near = jnp.where(in_doc, near, neg_fill)
            top = jnp.maximum(
                jnp.max(far, axis=1, keepdims=True), jnp.max(near, axis=1, keepdims=True)
            )
            far = jnp.exp2((far - top) * score_scale)
            near = jnp.exp2((near - top) * score_scale)
            total = jnp.sum(far, axis=1, keepdims=True) + jnp.sum(near, axis=1, keepdims=True)
            weighted = jnp.dot(
                far.astype(jnp.bfloat16), page_values, preferred_element_type=jnp.float32
            ) + jnp.dot(
                near.astype(jnp.bfloat16),
                qkv_ref[window, at : at + HD],
                preferred_element_type=jnp.float32,
            )
            out_ref[rows, cols] = (weighted / total).astype(jnp.bfloat16)


def column_block(exp_count, part, index):
    return (0, part * exp_count + index)


def pack_kernel(q_ref, k_ref, v_ref, out_ref):
    out_ref[...] = jnp.concatenate([q_ref[...], k_ref[...], v_ref[...]], axis=1)


def attention(qkv, q_gain, k_gain, pages, page_table, doc_len, doc_query):
    tok_count, width = qkv.shape[0], qkv.shape[1] // 3
    exp_count = lax.axis_size("exp")
    own = width // exp_count
    tokens = exp_count * tok_count
    parts = pl.pallas_call(
        pack_kernel,
        grid=(exp_count,),
        out_shape=jax.ShapeDtypeStruct((tokens, 3 * own), jnp.bfloat16),
        in_specs=[
            pl.BlockSpec((tok_count, own), functools.partial(column_block, exp_count, part))
            for part in range(3)
        ],
        out_specs=pl.BlockSpec((tok_count, 3 * own), lambda i: (i, 0)),
        name="pack_heads",
    )(qkv, qkv, qkv)
    group = lax.all_to_all(parts, "exp", split_axis=0, concat_axis=0, tiled=True)
    docs = doc_len.shape[1]
    spare = ((0, 0), (0, LANES - docs))
    out = pl.pallas_call(
        attention_kernel,
        out_shape=jax.ShapeDtypeStruct((tokens, own), jnp.bfloat16),
        scratch_shapes=[
            pltpu.VMEM((tokens, own), jnp.bfloat16),
            pltpu.VMEM((tokens, own), jnp.bfloat16),
        ],
        compiler_params=pltpu.CompilerParams(vmem_limit_bytes=32 * 1024 * 1024),
        name="paged_attention",
    )(
        group,
        pages.reshape(-1, 2 * own),
        jnp.pad(doc_len, spare),
        jnp.pad(doc_query, spare, constant_values=-1),
        page_table.reshape(-1, 1),
        q_gain.reshape(1, HD),
        k_gain.reshape(1, HD),
        jnp.asarray(rope_table()),
    )
    back = lax.all_to_all(out, "exp", split_axis=0, concat_axis=0, tiled=True)
    return back.reshape(exp_count, tok_count, own)


def expert_kernel(rows_ref, scale_ref, gate_ref, up_ref, down_ref, out_ref):
    rows = rows_ref[...]
    gate_act = jnp.dot(rows, gate_ref[0], preferred_element_type=jnp.float32)
    up_act = jnp.dot(rows, up_ref[0], preferred_element_type=jnp.float32)
    hidden_act = jax.nn.silu(gate_act) * (up_act * scale_ref[...])
    out_ref[...] = jnp.dot(
        hidden_act.astype(jnp.bfloat16), down_ref[0], preferred_element_type=jnp.float32
    ).astype(jnp.bfloat16)


def weighted_piece(rows, scale, gate_weight, up_weight, down_weight):
    count, width = rows.shape
    hidden = gate_weight.shape[2]
    tile = 256
    once = pl.Buffered(1)
    return pl.pallas_call(
        expert_kernel,
        grid=(count // tile,),
        out_shape=jax.ShapeDtypeStruct(rows.shape, jnp.bfloat16),
        in_specs=[
            pl.BlockSpec((tile, width), lambda i: (i, 0)),
            pl.BlockSpec((tile, 1), lambda i: (i, 0)),
            pl.BlockSpec((1, width, hidden), lambda i: (0, 0, 0), pipeline_mode=once),
            pl.BlockSpec((1, width, hidden), lambda i: (0, 0, 0), pipeline_mode=once),
            pl.BlockSpec((1, hidden, width), lambda i: (0, 0, 0), pipeline_mode=once),
        ],
        out_specs=pl.BlockSpec((tile, width), lambda i: (i, 0)),
        compiler_params=pltpu.CompilerParams(vmem_limit_bytes=24 * 1024 * 1024),
        cost_estimate=pl.CostEstimate(
            flops=6 * count * width * hidden,
            bytes_accessed=4 * count * width + 6 * width * hidden,
            transcendentals=count * hidden,
        ),
        name="expert_half",
    )(rows, scale, gate_weight, up_weight, down_weight)


def expert_piece(rows, gate_weight, up_weight, down_weight):
    gate_act = jnp.dot(rows, gate_weight[0], preferred_element_type=jnp.float32)
    up_act = jnp.dot(rows, up_weight[0], preferred_element_type=jnp.float32)
    hidden_act = jax.nn.silu(gate_act) * up_act
    piece_out = jnp.dot(
        hidden_act.astype(jnp.bfloat16), down_weight[0], preferred_element_type=jnp.float32
    )
    return piece_out.astype(jnp.bfloat16)


def slot_numbers(route_flat, bin_count):
    onehot = (route_flat[:, None] == jnp.arange(bin_count, dtype=jnp.int32)[None, :]).astype(
        jnp.int32
    )
    prior_count = jnp.cumsum(onehot, axis=0, dtype=jnp.int32) - onehot
    return jnp.sum(prior_count * onehot, axis=1, dtype=jnp.int32)


def experts_by_slots(normed, routes, route_weight, gate_weight, up_weight, down_weight):
    tok_count, width = normed.shape
    devices = lax.axis_size("req") * lax.axis_size("exp")
    experts = devices // 2
    capacity = 2 * max(1, 3 * tok_count * TOP // (4 * experts))
    route_flat = routes.reshape(-1)
    slots = slot_numbers(route_flat, experts)
    place = route_flat * capacity + slots
    token_ids = jnp.arange(tok_count * TOP, dtype=jnp.int32) // TOP
    slot_tokens = jnp.full((experts * capacity,), tok_count, jnp.int32).at[place].set(token_ids)
    padded_rows = jnp.concatenate([normed, jnp.zeros((1, width), jnp.bfloat16)], axis=0)
    outgoing = padded_rows[slot_tokens].reshape(experts, capacity, width)
    doubled = jnp.broadcast_to(outgoing[:, None], (experts, 2, capacity, width)).reshape(
        2 * experts, capacity, width
    )
    arrived = lax.all_to_all(doubled, ALL, split_axis=0, concat_axis=0, tiled=True)
    pieces = expert_piece(arrived.reshape(-1, width), gate_weight, up_weight, down_weight)
    returned = lax.all_to_all(
        pieces.reshape(arrived.shape), ALL, split_axis=0, concat_axis=0, tiled=True
    ).reshape(experts, 2, capacity, width)
    results = (returned[:, 0].astype(jnp.float32) + returned[:, 1].astype(jnp.float32)).astype(
        jnp.bfloat16
    )
    picked = results.reshape(experts * capacity, width)[place].reshape(tok_count, TOP, width)
    return jnp.einsum("tk,tkd->td", route_weight, picked.astype(jnp.float32))


GRID = (2, 2, 4)


def device_number(x, y, z, core):
    return ((y * 2 + core) * GRID[2] + z) * GRID[0] + x


def pairs(target):
    found = []
    for y in range(GRID[1]):
        for core in range(2):
            for z in range(GRID[2]):
                for x in range(GRID[0]):
                    to = target(x, y, z, core)
                    if to is not None:
                        found.append((device_number(x, y, z, core), device_number(*to)))
    return found


def move(block, target):
    return lax.ppermute(block, ALL, pairs(target))


def over_x(x, y, z, core):
    return (1 - x, y, z, core)


def over_y(x, y, z, core):
    return (x, 1 - y, z, core)


def over_core(x, y, z, core):
    return (x, y, z, 1 - core)


def z_pair(x, y, z, core):
    return (x, y, z ^ 1, core)


def z_far(x, y, z, core):
    return (x, y, z ^ 2, core)


def z_middle(x, y, z, core):
    return (x, y, 3 - z, core) if z in (1, 2) else None


def z_outward(x, y, z, core):
    return (x, y, {1: 0, 2: 3}[z], core) if z in (1, 2) else None


def z_inward(x, y, z, core):
    return (x, y, {0: 1, 3: 2}[z], core) if z in (0, 3) else None


def experts_dense(normed, routes, route_weight, gate_weight, up_weight, down_weight):
    f32 = jnp.float32
    tok_count = normed.shape[0]
    req, exp = lax.axis_index("req"), lax.axis_index("exp")
    z = exp // GRID[0]
    devices = lax.axis_size("req") * lax.axis_size("exp")
    experts = devices // 2
    chosen = routes.T[None] == jnp.arange(experts, dtype=jnp.int32)[:, None, None]
    dense = jnp.sum(jnp.where(chosen, route_weight.T[None], 0.0), axis=1)
    for target in (z_pair, z_far, over_x, over_y, over_core):
        dense = jnp.stack([dense, move(dense, target)])
    own_expert = (req * lax.axis_size("exp") + exp) // 2
    weights = lax.dynamic_index_in_dim(dense, own_expert, 5, False)

    is_middle = (z == 1) | (z == 2)
    slot_0 = normed
    slot_1 = move(slot_0, z_pair)
    middle = move(slot_0, z_middle)
    slot_2 = jnp.where(is_middle, move(slot_1, z_middle), move(middle, z_outward))
    slot_3 = jnp.where(is_middle, middle, move(slot_2, z_outward))

    partials = []
    for low, near, far in ((0, slot_0, slot_1), (2, slot_2, slot_3)):
        own = jnp.concatenate([near, far], axis=0)
        by_x = move(own, over_x)
        by_y = move(own, over_y)
        diagonal_near = move(by_x[:tok_count], over_y)
        diagonal_far = move(by_y[tok_count:], over_x)
        rows = jnp.concatenate([own, by_x, by_y, diagonal_near, diagonal_far], axis=0)
        other_rows = move(rows, over_core)
        results = []
        for side, held in ((1, other_rows), (0, rows)):
            scale = weights[side, :, :, low // 2].reshape(-1, 1)
            results.append(weighted_piece(held, scale, gate_weight, up_weight, down_weight))
        partials.append(results)

    def total(*terms):
        result = terms[0].astype(f32)
        for term in terms[1:]:
            result = result + term.astype(f32)
        return result

    def to_wire(value):
        return value.astype(jnp.bfloat16)

    sums = {}
    n = tok_count
    for low, (theirs, mine) in ((2, partials[1]), (0, partials[0])):
        came = move(theirs, over_core)

        def both(first, last):
            return total(mine[first * n : last * n], came[first * n : last * n])

        from_y = move(to_wire(both(6, 7)), over_y)
        from_x = move(to_wire(both(7, 8)), over_x)
        to_x = jnp.concatenate([to_wire(both(2, 3) + total(from_y)), to_wire(both(3, 4))], axis=0)
        to_y = jnp.concatenate([to_wire(both(4, 5)), to_wire(both(5, 6) + total(from_x))], axis=0)
        back_x, back_y = move(to_x, over_x), move(to_y, over_y)
        own = both(0, 2) + total(back_x) + total(back_y)
        sums[low], sums[low + 1] = own[:n], own[n:]

    sum_2 = sums[2] + total(move(to_wire(sums[3]), z_inward))
    sum_3 = sums[3] + total(move(to_wire(sums[2]), z_inward))
    sum_1 = sums[1] + total(move(to_wire(sum_2), z_middle))
    return sums[0] + total(move(to_wire(sum_3), z_middle)) + total(move(to_wire(sum_1), z_pair))


def local(
    hidden_in,
    qkv,
    q_gain,
    k_gain,
    query_pages,
    page_table,
    doc_lengths,
    doc_query,
    out_weight,
    moe_gain,
    routes,
    route_weight,
    gate_weight,
    up_weight,
    down_weight,
    score_weight,
):
    tok_count = hidden_in.shape[0]
    exp_index = lax.axis_index("exp")
    attn = attention(qkv, q_gain, k_gain, query_pages, page_table, doc_lengths, doc_query)
    attn = attn.transpose(1, 0, 2).reshape(hidden_in.shape)
    mixed = jnp.dot(attn, out_weight, preferred_element_type=jnp.float32)
    resid = (hidden_in.astype(jnp.float32) + mixed).astype(jnp.bfloat16)
    normed = rms_scale(resid.astype(jnp.float32), moe_gain).astype(jnp.bfloat16)
    is_small = (lax.axis_size("req"), lax.axis_size("exp")) == (2 * GRID[1], GRID[0] * GRID[2])
    moe = experts_dense if is_small else experts_by_slots
    combined = moe(normed, routes, route_weight, gate_weight, up_weight, down_weight)
    layer_out = (resid.astype(jnp.float32) + combined).astype(jnp.bfloat16)
    token_score = jnp.dot(
        layer_out.astype(jnp.float32), score_weight, precision=lax.Precision.HIGHEST
    )
    doc_len = doc_lengths[0]
    doc_ends = jnp.cumsum(doc_len, dtype=jnp.int32)
    own_pos = exp_index * tok_count + jnp.arange(tok_count, dtype=jnp.int32)
    member = (own_pos[:, None] < doc_ends[None, :]) & (
        own_pos[:, None] >= (doc_ends - doc_len)[None, :]
    )
    doc_partial = jnp.dot(
        token_score, member.astype(jnp.float32), precision=lax.Precision.HIGHEST
    )
    doc_sums = lax.psum(doc_partial, "exp")
    doc_scores = (doc_sums / doc_len.astype(jnp.float32))[None, :]
    return (layer_out, doc_scores)


def solution(mesh):
    in_specs = (
        P(("req", "exp"), None),
        P(("req", "exp"), None),
        P(),
        P(),
        P("req", None, None, "exp"),
        P("req", None),
        P("req", None),
        P("req", None),
        P(),
        P(),
        P(("req", "exp"), None),
        P(("req", "exp"), None),
        P(("req", "exp"), None, None),
        P(("req", "exp"), None, None),
        P(("req", "exp"), None, None),
        P(),
    )
    out_specs = (P(("req", "exp"), None), P("req", None))
    return jax.shard_map(local, mesh=mesh, in_specs=in_specs, out_specs=out_specs, check_vma=False)
```

```python
import functools

import jax
import jax.numpy as jnp
import numpy as np
from jax import lax
from jax.experimental import pallas as pl
from jax.experimental.pallas import tpu as pltpu
from jax.sharding import PartitionSpec as P

HEADS = 16
HD = 128
TOP = 8
PAGE = 128
LANES = 128
ALL = ("req", "exp")


eps = 1e-06
rope_base = 50000.0
neg_fill = -1e30


def rms_scale(values, gain_vec):
    mean_sq = jnp.mean(values * values, axis=-1, keepdims=True)
    return values * lax.rsqrt(mean_sq + eps) * gain_vec


def rope_table():
    half_dim = HD // 2
    frequency = rope_base ** (-(np.arange(half_dim) * 2.0 / HD))
    angles = (PAGE + np.arange(PAGE))[:, None] * frequency[None, :]
    cosine, sine = np.cos(angles), np.sin(angles)
    rest = np.concatenate([cosine, cosine, -sine, sine], axis=1).astype(np.float32)
    terms = []
    for _ in range(3):
        term = rest.astype(jnp.bfloat16)
        terms.append(term)
        rest = rest - term.astype(np.float32)
    return np.concatenate(terms, axis=1)


def attention_kernel(
    qkv_ref, pages_ref, len_ref, query_ref, table_ref, q_gain_ref, k_gain_ref, rope_ref,
    out_ref, q_rows, k_rows,
):
    tokens = qkv_ref.shape[0]
    heads = qkv_ref.shape[1] // (3 * HD)
    blocks = tokens // LANES
    keys = pages_ref.shape[0]
    score_scale = HD ** (-0.5) * 1.4426950408889634

    row_ids = lax.broadcasted_iota(jnp.int32, (LANES, LANES), 0)
    lane_ids = lax.broadcasted_iota(jnp.int32, (LANES, LANES), 1)
    lane_f32 = lane_ids.astype(jnp.float32)
    upper = (row_ids <= lane_ids).astype(jnp.bfloat16)
    lens = jnp.broadcast_to(len_ref[...].astype(jnp.bfloat16), (16, LANES))
    ends = jnp.dot(lens, upper, preferred_element_type=jnp.float32)[0:1]
    slot = lax.broadcasted_iota(jnp.int32, (table_ref.shape[0], LANES), 0)
    doc_page = jnp.sum(
        jnp.where(slot == query_ref[...], table_ref[...], 0).astype(jnp.float32),
        axis=0, keepdims=True,
    )

    def places(block):
        own = (row_ids + block * LANES).astype(jnp.float32)
        passed = own >= ends
        start = jnp.max(jnp.where(passed, ends, 0.0), axis=1, keepdims=True)
        stop = jnp.min(jnp.where(passed, 1e9, ends), axis=1, keepdims=True)
        doc = jnp.sum(passed.astype(jnp.float32), axis=1, keepdims=True)
        page = jnp.sum(jnp.where(lane_f32 == doc, doc_page, 0.0), axis=1, keepdims=True)
        return own, start, stop, page

    @pl.loop(0, blocks)
    def _(block):
        rows = pl.ds(pl.multiple_of(block * LANES, LANES), LANES)
        own, start, _, _ = places(block)
        onehot = (lane_f32 == own - start).astype(jnp.bfloat16)
        terms = jnp.dot(onehot, rope_ref[...], preferred_element_type=jnp.float32)
        both = terms[:, : 2 * HD] + (terms[:, 2 * HD : 4 * HD] + terms[:, 4 * HD :])
        cosine, sine = both[:, :HD], both[:, HD:]
        for part, gain_ref, kept in ((0, q_gain_ref, q_rows), (1, k_gain_ref, k_rows)):
            for head in range(heads):
                at = (part * heads + head) * HD
                values = qkv_ref[rows, at : at + HD].astype(jnp.float32)
                values = rms_scale(values, gain_ref[...])
                swapped = pltpu.roll(values, HD // 2, 1)
                kept[rows, head * HD : (head + 1) * HD] = (
                    values * cosine + swapped * sine
                ).astype(jnp.bfloat16)

    page_of_key = (
        lax.broadcasted_iota(jnp.int32, (LANES, keys), 1) // PAGE
    ).astype(jnp.float32)
    wide = 3 * LANES
    key_at = lax.broadcasted_iota(jnp.int32, (LANES, wide), 1)

    @pl.loop(0, blocks)
    def _(block):
        rows = pl.ds(pl.multiple_of(block * LANES, LANES), LANES)
        first = pl.multiple_of(jnp.clip(block - 1, 0, blocks - 3) * LANES, LANES)
        window = pl.ds(first, wide)
        _, start, stop, page = places(block)
        position = (key_at + first).astype(jnp.float32)
        in_page = page_of_key == page
        in_doc = (position >= start) & (position < stop)
        for head in range(heads):
            cols = slice(head * HD, (head + 1) * HD)
            query = q_rows[rows, cols]
            page_keys = pages_ref[:, 2 * head * HD : (2 * head + 1) * HD]
            page_values = pages_ref[:, (2 * head + 1) * HD : (2 * head + 2) * HD]
            at = (2 * heads + head) * HD
            contract = (((1,), (1,)), ((), ()))
            far = lax.dot_general(
                query, page_keys, contract, preferred_element_type=jnp.float32
            )
            near = lax.dot_general(
                query, k_rows[window, cols], contract, preferred_element_type=jnp.float32
            )
            far = jnp.where(in_page, far, neg_fill)
            near = jnp.where(in_doc, near, neg_fill)
            top = jnp.maximum(
                jnp.max(far, axis=1, keepdims=True), jnp.max(near, axis=1, keepdims=True)
            )
            far = jnp.exp2((far - top) * score_scale)
            near = jnp.exp2((near - top) * score_scale)
            total = jnp.sum(far, axis=1, keepdims=True) + jnp.sum(near, axis=1, keepdims=True)
            weighted = jnp.dot(
                far.astype(jnp.bfloat16), page_values, preferred_element_type=jnp.float32
            ) + jnp.dot(
                near.astype(jnp.bfloat16),
                qkv_ref[window, at : at + HD],
                preferred_element_type=jnp.float32,
            )
            out_ref[rows, cols] = (weighted / total).astype(jnp.bfloat16)


def pack_kernel(exp_count, qkv_ref, out_ref):
    rows = qkv_ref.shape[0]
    own = qkv_ref.shape[1] // (3 * exp_count)
    for index in range(exp_count):
        for part in range(3):
            at = (part * exp_count + index) * own
            out_ref[index * rows : (index + 1) * rows, part * own : (part + 1) * own] = qkv_ref[
                :, at : at + own
            ]


def attention(qkv, q_gain, k_gain, pages, page_table, doc_len, doc_query):
    tok_count, width = qkv.shape[0], qkv.shape[1] // 3
    exp_count = lax.axis_size("exp")
    own = width // exp_count
    tokens = exp_count * tok_count
    parts = pl.pallas_call(
        functools.partial(pack_kernel, exp_count),
        out_shape=jax.ShapeDtypeStruct((tokens, 3 * own), jnp.bfloat16),
        name="pack_heads",
    )(qkv)
    group = lax.all_to_all(parts, "exp", split_axis=0, concat_axis=0, tiled=True)
    docs = doc_len.shape[1]
    spare = ((0, 0), (0, LANES - docs))
    out = pl.pallas_call(
        attention_kernel,
        out_shape=jax.ShapeDtypeStruct((tokens, own), jnp.bfloat16),
        scratch_shapes=[
            pltpu.VMEM((tokens, own), jnp.bfloat16),
            pltpu.VMEM((tokens, own), jnp.bfloat16),
        ],
        compiler_params=pltpu.CompilerParams(vmem_limit_bytes=32 * 1024 * 1024),
        name="paged_attention",
    )(
        group,
        pages.reshape(-1, 2 * own),
        jnp.pad(doc_len, spare),
        jnp.pad(doc_query, spare, constant_values=-1),
        page_table.reshape(-1, 1),
        q_gain.reshape(1, HD),
        k_gain.reshape(1, HD),
        jnp.asarray(rope_table()),
    )
    back = lax.all_to_all(out, "exp", split_axis=0, concat_axis=0, tiled=True)
    return back.reshape(exp_count, tok_count, own)


def expert_kernel(
    steps, other_ref, rows_ref, scale_ref, gate_ref, up_ref, down_ref, relevance_ref,
    theirs_ref, mine_ref, their_score_ref, my_score_ref,
):
    def work(held_ref, out_ref, score_ref):
        held = held_ref[...]
        gate_act = jnp.dot(held, gate_ref[0], preferred_element_type=jnp.float32)
        up_act = jnp.dot(held, up_ref[0], preferred_element_type=jnp.float32)
        hidden_act = jax.nn.silu(gate_act) * (up_act * scale_ref[...])
        out_ref[...] = jnp.dot(
            hidden_act.astype(jnp.bfloat16), down_ref[0], preferred_element_type=jnp.float32
        ).astype(jnp.bfloat16)
        score_ref[...] = jnp.sum(hidden_act * relevance_ref[...], axis=1, keepdims=True)

    step = pl.program_id(0)

    @pl.when(step < steps)
    def _():
        work(other_ref, theirs_ref, their_score_ref)

    @pl.when(step >= steps)
    def _():
        work(rows_ref, mine_ref, my_score_ref)


def weighted_pieces(other, rows, scale, at, gate_weight, up_weight, down_weight, relevance):
    count, width = rows.shape
    hidden = gate_weight.shape[2]
    tile = 256 if count % 256 == 0 else 128
    steps = count // tile
    once = pl.Buffered(1)

    def early(i):
        return (jnp.minimum(i, steps - 1), 0)

    def late(i):
        return (jnp.maximum(i - steps, 0), 0)

    def place(i):
        return (jnp.where(i < steps, at[0] // tile + i, at[1] // tile + i - steps), 0)

    return pl.pallas_call(
        functools.partial(expert_kernel, steps),
        grid=(2 * steps,),
        out_shape=(
            jax.ShapeDtypeStruct(rows.shape, jnp.bfloat16),
            jax.ShapeDtypeStruct(rows.shape, jnp.bfloat16),
            jax.ShapeDtypeStruct((count, 1), jnp.float32),
            jax.ShapeDtypeStruct((count, 1), jnp.float32),
        ),
        in_specs=[
            pl.BlockSpec((tile, width), early),
            pl.BlockSpec((tile, width), late),
            pl.BlockSpec((tile, 1), place),
            pl.BlockSpec((1, width, hidden), lambda i: (0, 0, 0), pipeline_mode=once),
            pl.BlockSpec((1, width, hidden), lambda i: (0, 0, 0), pipeline_mode=once),
            pl.BlockSpec((1, hidden, width), lambda i: (0, 0, 0), pipeline_mode=once),
            pl.BlockSpec((1, hidden), lambda i: (0, 0)),
        ],
        out_specs=(
            pl.BlockSpec((tile, width), early),
            pl.BlockSpec((tile, width), late),
            pl.BlockSpec((tile, 1), early),
            pl.BlockSpec((tile, 1), late),
        ),
        compiler_params=pltpu.CompilerParams(vmem_limit_bytes=24 * 1024 * 1024),
        cost_estimate=pl.CostEstimate(
            flops=12 * count * width * hidden,
            bytes_accessed=8 * count * width + 6 * width * hidden,
            transcendentals=2 * count * hidden,
        ),
        name="expert_half",
    )(other, rows, scale, gate_weight, up_weight, down_weight, relevance)


def expert_piece(rows, gate_weight, up_weight, down_weight):
    gate_act = jnp.dot(rows, gate_weight[0], preferred_element_type=jnp.float32)
    up_act = jnp.dot(rows, up_weight[0], preferred_element_type=jnp.float32)
    hidden_act = jax.nn.silu(gate_act) * up_act
    piece_out = jnp.dot(
        hidden_act.astype(jnp.bfloat16), down_weight[0], preferred_element_type=jnp.float32
    )
    return piece_out.astype(jnp.bfloat16)


def slot_numbers(route_flat, bin_count):
    onehot = (route_flat[:, None] == jnp.arange(bin_count, dtype=jnp.int32)[None, :]).astype(
        jnp.int32
    )
    prior_count = jnp.cumsum(onehot, axis=0, dtype=jnp.int32) - onehot
    return jnp.sum(prior_count * onehot, axis=1, dtype=jnp.int32)


def experts_by_slots(normed, routes, route_weight, gate_weight, up_weight, down_weight):
    tok_count, width = normed.shape
    devices = lax.axis_size("req") * lax.axis_size("exp")
    experts = devices // 2
    capacity = 2 * max(1, 3 * tok_count * TOP // (4 * experts))
    route_flat = routes.reshape(-1)
    slots = slot_numbers(route_flat, experts)
    place = route_flat * capacity + slots
    token_ids = jnp.arange(tok_count * TOP, dtype=jnp.int32) // TOP
    slot_tokens = jnp.full((experts * capacity,), tok_count, jnp.int32).at[place].set(token_ids)
    padded_rows = jnp.concatenate([normed, jnp.zeros((1, width), jnp.bfloat16)], axis=0)
    outgoing = padded_rows[slot_tokens].reshape(experts, capacity, width)
    doubled = jnp.broadcast_to(outgoing[:, None], (experts, 2, capacity, width)).reshape(
        2 * experts, capacity, width
    )
    arrived = lax.all_to_all(doubled, ALL, split_axis=0, concat_axis=0, tiled=True)
    pieces = expert_piece(arrived.reshape(-1, width), gate_weight, up_weight, down_weight)
    returned = lax.all_to_all(
        pieces.reshape(arrived.shape), ALL, split_axis=0, concat_axis=0, tiled=True
    ).reshape(experts, 2, capacity, width)
    results = (returned[:, 0].astype(jnp.float32) + returned[:, 1].astype(jnp.float32)).astype(
        jnp.bfloat16
    )
    picked = results.reshape(experts * capacity, width)[place].reshape(tok_count, TOP, width)
    return jnp.einsum("tk,tkd->td", route_weight, picked.astype(jnp.float32))


GRID = (2, 2, 4)


def device_number(x, y, z, core):
    return ((y * 2 + core) * GRID[2] + z) * GRID[0] + x


def pairs(target):
    found = []
    for y in range(GRID[1]):
        for core in range(2):
            for z in range(GRID[2]):
                for x in range(GRID[0]):
                    to = target(x, y, z, core)
                    if to is not None:
                        found.append((device_number(x, y, z, core), device_number(*to)))
    return found


def move(block, target):
    return lax.ppermute(block, ALL, pairs(target))


def over_x(x, y, z, core):
    return (1 - x, y, z, core)


def over_y(x, y, z, core):
    return (x, 1 - y, z, core)


def over_core(x, y, z, core):
    return (x, y, z, 1 - core)


def z_pair(x, y, z, core):
    return (x, y, z ^ 1, core)


def z_far(x, y, z, core):
    return (x, y, z ^ 2, core)


def z_middle(x, y, z, core):
    return (x, y, 3 - z, core) if z in (1, 2) else None


def z_outward(x, y, z, core):
    return (x, y, {1: 0, 2: 3}[z], core) if z in (1, 2) else None


def z_inward(x, y, z, core):
    return (x, y, {0: 1, 3: 2}[z], core) if z in (0, 3) else None


def together(*values):
    return lax.optimization_barrier(values)


def route_table(routes, route_weight):
    exp_count = lax.axis_size("exp")
    experts = lax.axis_size("req") * exp_count // 2
    chosen = routes.T[None] == jnp.arange(experts, dtype=jnp.int32)[:, None, None]
    dense = jnp.sum(jnp.where(chosen, route_weight.T[None], 0.0), axis=1)
    for target in (z_pair, z_far, over_x, over_y, over_core):
        dense = jnp.stack([dense, move(dense, target)])
    own_expert = (lax.axis_index("req") * exp_count + lax.axis_index("exp")) // 2
    return lax.dynamic_index_in_dim(dense, own_expert, 5, False)


def member_table(doc_len, tok_count):
    ends = jnp.cumsum(doc_len, dtype=jnp.int32)
    bounds = jnp.stack([ends - doc_len, ends])
    for target in (over_y, over_core):
        bounds = jnp.stack([bounds, move(bounds, target)])
    exp = lax.axis_index("exp")
    flips = np.array([[[k1 * 4 + k0 * 2 + dx for k0 in (0, 1)] for k1 in (0, 1)] for dx in (0, 1)])
    blocks = jnp.bitwise_xor(exp, jnp.asarray(flips, jnp.int32))
    position = blocks[..., None] * tok_count + jnp.arange(tok_count, dtype=jnp.int32)
    position = position[None, None, ..., None]

    def spread(side):
        return bounds[:, :, side][:, :, None, None, None, None, :]

    return ((position >= spread(0)) & (position < spread(1))).astype(jnp.float32)


def experts_dense(resid, normed, weights, member, gate_weight, up_weight, down_weight, score_weight):
    f32 = jnp.float32
    n = normed.shape[0]
    h = n // 2
    z = lax.axis_index("exp") // GRID[0]
    middle = (z == 1) | (z == 2)
    relevance = jnp.dot(
        down_weight[0].astype(f32), score_weight, precision=lax.Precision.HIGHEST
    )[None]
    scale = weights.transpose(3, 4, 0, 1, 2, 5).reshape(-1, 1)
    normed, scale, member, relevance = together(normed, scale, member, relevance)

    def join(*blocks):
        return jnp.concatenate(blocks, axis=0)

    def work(slot, first, other, rows):
        at = [(slot * 2 + side) * 4 * n + first for side in (1, 0)]
        return weighted_pieces(
            other, rows, scale, at, gate_weight, up_weight, down_weight, relevance
        )

    p, m = move(normed, z_pair), move(normed, z_middle)
    x0, y0 = move(normed, over_x), move(normed, over_y)
    p, m, x0, y0 = together(p, m, x0, y0)

    by_x, by_y = move(join(p, y0[h:]), over_x), move(join(p, x0[:h]), over_y)
    q_middle, q_end = move(p, z_middle), move(m, z_outward)
    by_x, by_y, q_middle, q_end = together(by_x, by_y, q_middle, q_end)
    q = jnp.where(middle, q_middle, q_end)
    xp, yp = by_x[:n], by_y[:n]
    rows_0 = join(normed, x0, y0, by_y[n:], by_x[n:])

    by_x, by_y = move(join(q, yp[h:]), over_x), move(join(q, xp[:h]), over_y)
    r_end = move(q, z_outward)
    out_0 = work(0, 0, move(rows_0, over_core), rows_0)
    by_x, by_y, r_end, out_0 = together(by_x, by_y, r_end, out_0)
    r = jnp.where(middle, m, r_end)
    xq, yq = by_x[:n], by_y[:n]
    rows_p = join(p, xp, yp, by_y[n:], by_x[n:])

    by_x, by_y = move(join(r, yq[h:]), over_x), move(join(r, xq[:h]), over_y)
    out_p = work(1, 0, move(rows_p, over_core), rows_p)
    by_x, by_y, out_p = together(by_x, by_y, out_p)
    xr, yr = by_x[:n], by_y[:n]
    rows_q = join(q, xq, yq, by_y[n:], by_x[n:])

    by_x, by_y = move(yr[h:], over_x), move(xr[:h], over_y)
    rows_r = join(r, xr, yr)
    other_q, other_r = move(rows_q, over_core), move(rows_r, over_core)
    by_x, by_y, other_r = together(by_x, by_y, other_r)
    rows_d = join(by_y, by_x)
    out_d = work(3, 3 * n, move(rows_d, over_core), rows_d)
    out_q = work(2, 0, other_q, rows_q)
    out_r = work(3, 0, other_r, rows_r)

    def total(*terms):
        result = terms[0].astype(f32)
        for term in terms[1:]:
            result = result + term.astype(f32)
        return result

    def to_wire(value):
        return value.astype(jnp.bfloat16)

    class Plane:
        def __init__(self, mine, came):
            self.mine, self.came = mine, came

        def part(self, first, last):
            return total(self.mine[first:last], self.came[first:last])

        def diagonal(self, at=3):
            ends = to_wire(self.part(at * n, (at + 1) * n))
            return ends[:h], ends[h:]

        def sides(self, from_y, from_x):
            of_x = join(self.part(n, n + h) + total(from_y), self.part(n + h, 2 * n))
            of_y = join(self.part(2 * n, 2 * n + h), self.part(2 * n + h, 3 * n) + total(from_x))
            return to_wire(of_x), to_wire(of_y)

        def own(self, *terms):
            return self.part(0, n) + total(*terms)

    d = Plane(out_d[1], move(out_d[0], over_core))
    to_y, to_x = d.diagonal(0)
    from_y, from_x = move(to_y, over_y), move(to_x, over_x)
    r = Plane(out_r[1], move(out_r[0], over_core))
    q = Plane(out_q[1], move(out_q[0], over_core))
    from_y, from_x, r.came, q.came = together(from_y, from_x, r.came, q.came)

    of_x, of_y = r.sides(from_y, from_x)
    to_y, to_x = q.diagonal()
    by_x, by_y = move(join(of_x, to_x), over_x), move(join(of_y, to_y), over_y)
    p = Plane(out_p[1], move(out_p[0], over_core))
    by_x, by_y, p.came = together(by_x, by_y, p.came)
    sum_r = r.own(by_x[:n], by_y[:n])

    of_x, of_y = q.sides(by_y[n:], by_x[n:])
    to_y, to_x = p.diagonal()
    by_x, by_y = move(join(of_x, to_x), over_x), move(join(of_y, to_y), over_y)
    q_more = move(to_wire(sum_r), z_inward)
    own = Plane(out_0[1], move(out_0[0], over_core))
    by_x, by_y, q_more, own.came = together(by_x, by_y, q_more, own.came)
    sum_q = to_wire(q.own(by_x[:n], by_y[:n], q_more))

    of_x, of_y = p.sides(by_y[n:], by_x[n:])
    to_y, to_x = own.diagonal()
    by_x, by_y = move(join(of_x, to_x), over_x), move(join(of_y, to_y), over_y)
    p_more, r_more = move(sum_q, z_middle), move(sum_q, z_inward)
    by_x, by_y, p_more, r_more = together(by_x, by_y, p_more, r_more)
    sum_p = p.own(by_x[:n], by_y[:n], p_more)
    sum_r = sum_r + total(r_more)

    of_x, of_y = own.sides(by_y[n:], by_x[n:])
    by_x, by_y = move(of_x, over_x), move(of_y, over_y)
    from_p, from_r = move(to_wire(sum_p), z_pair), move(to_wire(sum_r), z_middle)

    def score(out):
        return out[3], out[2]

    scores = jnp.stack(
        [jnp.stack(score(out)) for out in (out_0, out_p, out_q)]
        + [jnp.stack([join(*pair) for pair in zip(score(out_r), score(out_d))])]
    ).reshape(2, 2, 2, 2, 2, n)
    scores = scores.transpose(2, 3, 4, 0, 1, 5)
    own_score = jnp.dot(resid.astype(f32), score_weight, precision=lax.Precision.HIGHEST)
    doc_sums = jnp.sum(member * scores[..., None], axis=(2, 3, 4, 5))
    doc_sums = doc_sums.at[0, 0].add(jnp.sum(member[0, 0, 0, 0, 0] * own_score[:, None], axis=0))
    for target in (over_core, over_y):
        doc_sums = doc_sums[0] + move(doc_sums[1], target)
    for target in (over_x, z_pair, z_far):
        doc_sums = doc_sums + move(doc_sums, target)
    combined = own.own(by_x, by_y, from_p, from_r)
    return (resid.astype(f32) + combined).astype(jnp.bfloat16), doc_sums


def is_small():
    return (lax.axis_size("req"), lax.axis_size("exp")) == (2 * GRID[1], GRID[0] * GRID[2])


def local(
    hidden_in,
    qkv,
    q_gain,
    k_gain,
    query_pages,
    page_table,
    doc_lengths,
    doc_query,
    out_weight,
    moe_gain,
    routes,
    route_weight,
    gate_weight,
    up_weight,
    down_weight,
    score_weight,
):
    tok_count = hidden_in.shape[0]
    exp_index = lax.axis_index("exp")
    doc_len = doc_lengths[0]
    attn = attention(qkv, q_gain, k_gain, query_pages, page_table, doc_lengths, doc_query)
    attn = attn.transpose(1, 0, 2).reshape(hidden_in.shape)
    mixed = jnp.dot(attn, out_weight, preferred_element_type=jnp.float32)
    resid = (hidden_in.astype(jnp.float32) + mixed).astype(jnp.bfloat16)
    normed = rms_scale(resid.astype(jnp.float32), moe_gain).astype(jnp.bfloat16)
    if is_small():
        layer_out, doc_sums = experts_dense(
            resid,
            normed,
            route_table(routes, route_weight),
            member_table(doc_len, tok_count),
            gate_weight,
            up_weight,
            down_weight,
            score_weight,
        )
        return (layer_out, (doc_sums / doc_len.astype(jnp.float32))[None, :])
    combined = experts_by_slots(
        normed, routes, route_weight, gate_weight, up_weight, down_weight
    )
    layer_out = (resid.astype(jnp.float32) + combined).astype(jnp.bfloat16)
    token_score = jnp.dot(
        layer_out.astype(jnp.float32), score_weight, precision=lax.Precision.HIGHEST
    )
    doc_ends = jnp.cumsum(doc_len, dtype=jnp.int32)
    own_pos = exp_index * tok_count + jnp.arange(tok_count, dtype=jnp.int32)
    member = (own_pos[:, None] < doc_ends[None, :]) & (
        own_pos[:, None] >= (doc_ends - doc_len)[None, :]
    )
    doc_partial = jnp.dot(
        token_score, member.astype(jnp.float32), precision=lax.Precision.HIGHEST
    )
    doc_sums = lax.psum(doc_partial, "exp")
    doc_scores = (doc_sums / doc_len.astype(jnp.float32))[None, :]
    return (layer_out, doc_scores)


def solution(mesh):
    in_specs = (
        P(("req", "exp"), None),
        P(("req", "exp"), None),
        P(),
        P(),
        P("req", None, None, "exp"),
        P("req", None),
        P("req", None),
        P("req", None),
        P(),
        P(),
        P(("req", "exp"), None),
        P(("req", "exp"), None),
        P(("req", "exp"), None, None),
        P(("req", "exp"), None, None),
        P(("req", "exp"), None, None),
        P(),
    )
    out_specs = (P(("req", "exp"), None), P("req", None))
    return jax.shard_map(local, mesh=mesh, in_specs=in_specs, out_specs=out_specs, check_vma=False)
```

```python
import functools

import jax
import jax.numpy as jnp
import numpy as np
from jax import lax
from jax.experimental import pallas as pl
from jax.experimental.pallas import tpu as pltpu
from jax.sharding import PartitionSpec as P

HEADS = 16
HD = 128
TOP = 8
PAGE = 128
LANES = 128
ALL = ("req", "exp")


eps = 1e-06
rope_base = 50000.0
neg_fill = -1e30


def rms_scale(values, gain_vec):
    mean_sq = jnp.mean(values * values, axis=-1, keepdims=True)
    return values * lax.rsqrt(mean_sq + eps) * gain_vec


def rope_table():
    half_dim = HD // 2
    frequency = rope_base ** (-(np.arange(half_dim) * 2.0 / HD))
    angles = (PAGE + np.arange(PAGE))[:, None] * frequency[None, :]
    cosine, sine = np.cos(angles), np.sin(angles)
    rest = np.concatenate([cosine, cosine, -sine, sine], axis=1).astype(np.float32)
    terms = []
    for _ in range(3):
        term = rest.astype(jnp.bfloat16)
        terms.append(term)
        rest = rest - term.astype(np.float32)
    return np.concatenate(terms, axis=1)


def attention_kernel(
    qkv_ref, pages_ref, len_ref, query_ref, table_ref, q_gain_ref, k_gain_ref, rope_ref,
    out_ref, q_rows, k_rows,
):
    tokens = qkv_ref.shape[0]
    heads = qkv_ref.shape[1] // (3 * HD)
    blocks = tokens // LANES
    keys = pages_ref.shape[0]
    score_scale = HD ** (-0.5) * 1.4426950408889634

    row_ids = lax.broadcasted_iota(jnp.int32, (LANES, LANES), 0)
    lane_ids = lax.broadcasted_iota(jnp.int32, (LANES, LANES), 1)
    lane_f32 = lane_ids.astype(jnp.float32)
    upper = (row_ids <= lane_ids).astype(jnp.bfloat16)
    lens = jnp.broadcast_to(len_ref[...].astype(jnp.bfloat16), (16, LANES))
    ends = jnp.dot(lens, upper, preferred_element_type=jnp.float32)[0:1]
    slot = lax.broadcasted_iota(jnp.int32, (table_ref.shape[0], LANES), 0)
    doc_page = jnp.sum(
        jnp.where(slot == query_ref[...], table_ref[...], 0).astype(jnp.float32),
        axis=0, keepdims=True,
    )

    def places(block):
        own = (row_ids + block * LANES).astype(jnp.float32)
        passed = own >= ends
        start = jnp.max(jnp.where(passed, ends, 0.0), axis=1, keepdims=True)
        stop = jnp.min(jnp.where(passed, 1e9, ends), axis=1, keepdims=True)
        doc = jnp.sum(passed.astype(jnp.float32), axis=1, keepdims=True)
        page = jnp.sum(jnp.where(lane_f32 == doc, doc_page, 0.0), axis=1, keepdims=True)
        return own, start, stop, page

    @pl.loop(0, blocks)
    def _(block):
        rows = pl.ds(pl.multiple_of(block * LANES, LANES), LANES)
        own, start, _, _ = places(block)
        onehot = (lane_f32 == own - start).astype(jnp.bfloat16)
        terms = jnp.dot(onehot, rope_ref[...], preferred_element_type=jnp.float32)
        both = terms[:, : 2 * HD] + (terms[:, 2 * HD : 4 * HD] + terms[:, 4 * HD :])
        cosine, sine = both[:, :HD], both[:, HD:]
        for part, gain_ref, kept in ((0, q_gain_ref, q_rows), (1, k_gain_ref, k_rows)):
            for head in range(heads):
                at = (part * heads + head) * HD
                values = qkv_ref[rows, at : at + HD].astype(jnp.float32)
                values = rms_scale(values, gain_ref[...])
                swapped = pltpu.roll(values, HD // 2, 1)
                kept[rows, head * HD : (head + 1) * HD] = (
                    values * cosine + swapped * sine
                ).astype(jnp.bfloat16)

    page_of_key = (
        lax.broadcasted_iota(jnp.int32, (LANES, keys), 1) // PAGE
    ).astype(jnp.float32)
    wide = 3 * LANES
    key_at = lax.broadcasted_iota(jnp.int32, (LANES, wide), 1)

    @pl.loop(0, blocks)
    def _(block):
        rows = pl.ds(pl.multiple_of(block * LANES, LANES), LANES)
        first = pl.multiple_of(jnp.clip(block - 1, 0, blocks - 3) * LANES, LANES)
        window = pl.ds(first, wide)
        _, start, stop, page = places(block)
        position = (key_at + first).astype(jnp.float32)
        in_page = page_of_key == page
        in_doc = (position >= start) & (position < stop)
        for head in range(heads):
            cols = slice(head * HD, (head + 1) * HD)
            query = q_rows[rows, cols]
            page_keys = pages_ref[:, 2 * head * HD : (2 * head + 1) * HD]
            page_values = pages_ref[:, (2 * head + 1) * HD : (2 * head + 2) * HD]
            at = (2 * heads + head) * HD
            contract = (((1,), (1,)), ((), ()))
            far = lax.dot_general(
                query, page_keys, contract, preferred_element_type=jnp.float32
            )
            near = lax.dot_general(
                query, k_rows[window, cols], contract, preferred_element_type=jnp.float32
            )
            far = jnp.where(in_page, far, neg_fill)
            near = jnp.where(in_doc, near, neg_fill)
            top = jnp.maximum(
                jnp.max(far, axis=1, keepdims=True), jnp.max(near, axis=1, keepdims=True)
            )
            far = jnp.exp2((far - top) * score_scale)
            near = jnp.exp2((near - top) * score_scale)
            total = jnp.sum(far, axis=1, keepdims=True) + jnp.sum(near, axis=1, keepdims=True)
            weighted = jnp.dot(
                far.astype(jnp.bfloat16), page_values, preferred_element_type=jnp.float32
            ) + jnp.dot(
                near.astype(jnp.bfloat16),
                qkv_ref[window, at : at + HD],
                preferred_element_type=jnp.float32,
            )
            out_ref[rows, cols] = (weighted / total).astype(jnp.bfloat16)


def pack_kernel(exp_count, qkv_ref, out_ref):
    rows = qkv_ref.shape[0]
    own = qkv_ref.shape[1] // (3 * exp_count)
    for index in range(exp_count):
        for part in range(3):
            at = (part * exp_count + index) * own
            out_ref[index * rows : (index + 1) * rows, part * own : (part + 1) * own] = qkv_ref[
                :, at : at + own
            ]


def attention(qkv, q_gain, k_gain, pages, page_table, doc_len, doc_query, tables):
    tok_count, width = qkv.shape[0], qkv.shape[1] // 3
    exp_count = lax.axis_size("exp")
    own = width // exp_count
    tokens = exp_count * tok_count
    parts = pl.pallas_call(
        functools.partial(pack_kernel, exp_count),
        out_shape=jax.ShapeDtypeStruct((tokens, 3 * own), jnp.bfloat16),
        compiler_params=pltpu.CompilerParams(vmem_limit_bytes=8 * 1024 * 1024),
        name="pack_heads",
    )(qkv)
    group = lax.all_to_all(parts, "exp", split_axis=0, concat_axis=0, tiled=True)
    docs = doc_len.shape[1]
    spare = ((0, 0), (0, LANES - docs))
    out = pl.pallas_call(
        attention_kernel,
        out_shape=jax.ShapeDtypeStruct((tokens, own), jnp.bfloat16),
        scratch_shapes=[
            pltpu.VMEM((tokens, own), jnp.bfloat16),
            pltpu.VMEM((tokens, own), jnp.bfloat16),
        ],
        compiler_params=pltpu.CompilerParams(vmem_limit_bytes=14 * 1024 * 1024),
        name="paged_attention",
    )(
        group,
        pages.reshape(-1, 2 * own),
        jnp.pad(doc_len, spare),
        jnp.pad(doc_query, spare, constant_values=-1),
        page_table.reshape(-1, 1),
        q_gain.reshape(1, HD),
        k_gain.reshape(1, HD),
        jnp.asarray(rope_table()),
    )
    out, tables = lax.optimization_barrier((out, tables))
    back = lax.all_to_all(out, "exp", split_axis=0, concat_axis=0, tiled=True)
    return back.reshape(exp_count, tok_count, own), tables


def expert_kernel(sides, steps, first, held, *refs):
    rows_refs, refs = refs[:sides], refs[sides:]
    scale_ref, relevance_ref, *weight_refs = refs[:5]
    out_refs, score_ref = refs[5 : 5 + sides], refs[5 + sides]
    step = pl.program_id(0)
    per_tile = rows_refs[0].shape[0] // LANES
    if held:
        gate, up, down = (ref.at[0] for ref in weight_refs)
    else:
        gate, up, down, sems = refs[6 + sides :]
        copies = [
            pltpu.make_async_copy(source.at[0], target, sems.at[at])
            for at, (source, target) in enumerate(zip(weight_refs, (gate, up, down)))
        ]

    def work(rows_ref, out_ref, arriving):
        rows = rows_ref[...]
        if arriving:
            copies[0].wait()
        gate_act = jnp.dot(rows, gate[...], preferred_element_type=jnp.float32)
        if arriving:
            copies[1].wait()
        up_act = jnp.dot(rows, up[...], preferred_element_type=jnp.float32)
        spread = [
            jnp.broadcast_to(
                scale_ref[pl.ds(first + step * per_tile + part, 1)], (LANES, LANES)
            ).T
            for part in range(per_tile)
        ]
        scale = jnp.concatenate(spread, axis=0)
        scale = jnp.concatenate([scale] * (up_act.shape[1] // LANES), axis=1)
        hidden_act = (jax.nn.silu(gate_act) * (up_act * scale)).astype(jnp.bfloat16)
        score = lax.dot_general(
            relevance_ref[...], hidden_act, (((1,), (1,)), ((), ())),
            preferred_element_type=jnp.float32,
        )
        score = jnp.sum(score, axis=0, keepdims=True)
        for part in range(per_tile):
            score_ref[pl.ds(step * per_tile + part, 1)] = score[
                :, part * LANES : (part + 1) * LANES
            ]
        if arriving:
            copies[2].wait()
        out_ref[...] = jnp.dot(
            hidden_act, down[...], preferred_element_type=jnp.float32
        ).astype(jnp.bfloat16)

    if not held:

        @pl.when(step == 0)
        def _():
            for copy in copies:
                copy.start()
            work(rows_refs[0], out_refs[0], True)

    for side in range(sides):
        mine = step // steps == side
        if not held and side == 0:
            mine = mine & (step > 0)

        @pl.when(mine)
        def _():
            work(rows_refs[side], out_refs[side], False)


def weighted_pieces(rows, scale, first, relevance, weights, held):
    sides = len(rows)
    count, width = rows[0].shape
    hidden = weights[0].shape[2]
    tile = 256 if count % 256 == 0 else count
    steps = count // tile
    space = pltpu.VMEM if held else pltpu.HBM
    weights = [pltpu.with_memory_space_constraint(weight, space) for weight in weights]

    def rows_of(side):
        return pl.BlockSpec((tile, width), lambda i: (jnp.clip(i - side * steps, 0, steps - 1), 0))

    fetched = [pltpu.VMEM(weight.shape[1:], jnp.bfloat16) for weight in weights]
    kept = pltpu.HBM if held else jax.ShapeDtypeStruct
    return pl.pallas_call(
        functools.partial(expert_kernel, sides, steps, first, held),
        grid=(sides * steps,),
        out_shape=[kept((count, width), jnp.bfloat16)] * sides
        + [jax.ShapeDtypeStruct((sides * count // LANES, LANES), jnp.float32)],
        in_specs=[rows_of(side) for side in range(sides)]
        + [
            pl.BlockSpec(scale.shape, lambda i: (0, 0)),
            pl.BlockSpec(relevance.shape, lambda i: (0, 0)),
        ]
        + [pl.BlockSpec(memory_space=space)] * 3,
        out_specs=[rows_of(side) for side in range(sides)]
        + [pl.BlockSpec((sides * count // LANES, LANES), lambda i: (0, 0))],
        scratch_shapes=[] if held else fetched + [pltpu.SemaphoreType.DMA((3,))],
        compiler_params=pltpu.CompilerParams(
            vmem_limit_bytes=((14 if tile <= 256 else 19) + (0 if held else 7)) * 1024 * 1024
        ),
        cost_estimate=pl.CostEstimate(
            flops=6 * sides * count * width * hidden,
            bytes_accessed=4 * sides * count * width + 6 * width * hidden,
            transcendentals=sides * count * hidden,
        ),
        name="expert_half",
    )(*rows, scale, relevance, *weights)


def expert_piece(rows, gate_weight, up_weight, down_weight):
    gate_act = jnp.dot(rows, gate_weight[0], preferred_element_type=jnp.float32)
    up_act = jnp.dot(rows, up_weight[0], preferred_element_type=jnp.float32)
    hidden_act = jax.nn.silu(gate_act) * up_act
    piece_out = jnp.dot(
        hidden_act.astype(jnp.bfloat16), down_weight[0], preferred_element_type=jnp.float32
    )
    return piece_out.astype(jnp.bfloat16)


def slot_numbers(route_flat, bin_count):
    onehot = (route_flat[:, None] == jnp.arange(bin_count, dtype=jnp.int32)[None, :]).astype(
        jnp.int32
    )
    prior_count = jnp.cumsum(onehot, axis=0, dtype=jnp.int32) - onehot
    return jnp.sum(prior_count * onehot, axis=1, dtype=jnp.int32)


def experts_by_slots(normed, routes, route_weight, gate_weight, up_weight, down_weight):
    tok_count, width = normed.shape
    devices = lax.axis_size("req") * lax.axis_size("exp")
    experts = devices // 2
    capacity = 2 * max(1, 3 * tok_count * TOP // (4 * experts))
    route_flat = routes.reshape(-1)
    slots = slot_numbers(route_flat, experts)
    place = route_flat * capacity + slots
    token_ids = jnp.arange(tok_count * TOP, dtype=jnp.int32) // TOP
    slot_tokens = jnp.full((experts * capacity,), tok_count, jnp.int32).at[place].set(token_ids)
    padded_rows = jnp.concatenate([normed, jnp.zeros((1, width), jnp.bfloat16)], axis=0)
    outgoing = padded_rows[slot_tokens].reshape(experts, capacity, width)
    doubled = jnp.broadcast_to(outgoing[:, None], (experts, 2, capacity, width)).reshape(
        2 * experts, capacity, width
    )
    arrived = lax.all_to_all(doubled, ALL, split_axis=0, concat_axis=0, tiled=True)
    pieces = expert_piece(arrived.reshape(-1, width), gate_weight, up_weight, down_weight)
    returned = lax.all_to_all(
        pieces.reshape(arrived.shape), ALL, split_axis=0, concat_axis=0, tiled=True
    ).reshape(experts, 2, capacity, width)
    results = (returned[:, 0].astype(jnp.float32) + returned[:, 1].astype(jnp.float32)).astype(
        jnp.bfloat16
    )
    picked = results.reshape(experts * capacity, width)[place].reshape(tok_count, TOP, width)
    return jnp.einsum("tk,tkd->td", route_weight, picked.astype(jnp.float32))


GRID = (2, 2, 4)


def device_number(x, y, z, core):
    return ((y * 2 + core) * GRID[2] + z) * GRID[0] + x


def pairs(target):
    found = []
    for y in range(GRID[1]):
        for core in range(2):
            for z in range(GRID[2]):
                for x in range(GRID[0]):
                    to = target(x, y, z, core)
                    if to is not None:
                        found.append((device_number(x, y, z, core), device_number(*to)))
    return found


def move(block, target):
    return lax.ppermute(block, ALL, pairs(target))


def over_x(x, y, z, core):
    return (1 - x, y, z, core)


def over_y(x, y, z, core):
    return (x, 1 - y, z, core)


def over_core(x, y, z, core):
    return (x, y, z, 1 - core)


def z_pair(x, y, z, core):
    return (x, y, z ^ 1, core)


def z_far(x, y, z, core):
    return (x, y, z ^ 2, core)


def z_middle(x, y, z, core):
    return (x, y, 3 - z, core) if z in (1, 2) else None


def z_outward(x, y, z, core):
    return (x, y, {1: 0, 2: 3}[z], core) if z in (1, 2) else None


def z_inward(x, y, z, core):
    return (x, y, {0: 1, 3: 2}[z], core) if z in (0, 3) else None


def together(*values):
    return lax.optimization_barrier(values)


def start_tables(routes, route_weight):
    experts = lax.axis_size("req") * lax.axis_size("exp") // 2
    chosen = routes.T[None] == jnp.arange(experts, dtype=jnp.int32)[:, None, None]
    dense = jnp.sum(jnp.where(chosen, route_weight.T[None], 0.0), axis=1)
    for target in (z_pair, z_far):
        dense = jnp.stack([dense, move(dense, target)])
    return dense


def finish_tables(dense, doc_len):
    tok_count = dense.shape[-1]
    for target in (over_x, over_y, over_core):
        dense = jnp.stack([dense, move(dense, target)])
    exp = lax.axis_index("exp")
    own_expert = (lax.axis_index("req") * lax.axis_size("exp") + exp) // 2
    weights = lax.dynamic_index_in_dim(dense, own_expert, 5, False)
    ends = jnp.cumsum(doc_len, dtype=jnp.int32)
    bounds = jnp.stack([ends - doc_len, ends])
    for target in (over_y, over_core):
        bounds = jnp.stack([bounds, move(bounds, target)])
    flips = np.array([[[k1 * 4 + k0 * 2 + dx for k0 in (0, 1)] for k1 in (0, 1)] for dx in (0, 1)])
    blocks = jnp.bitwise_xor(exp, jnp.asarray(flips, jnp.int32))
    position = blocks[..., None] * tok_count + jnp.arange(tok_count, dtype=jnp.int32)
    position = position[None, None, ..., None, :]

    def spread(side):
        return bounds[:, :, side][:, :, None, None, None, :, None]

    return weights, ((position >= spread(0)) & (position < spread(1))).astype(jnp.float32)


def hold_kernel(*refs):
    count = (len(refs) - 1) // 2
    copies = [
        pltpu.make_async_copy(refs[at], refs[count + at], refs[-1].at[at]) for at in range(count)
    ]
    for copy in copies:
        copy.start()
    for copy in copies:
        copy.wait()


def hold(*arrays):
    return pl.pallas_call(
        hold_kernel,
        out_shape=[pltpu.VMEM(array.shape, array.dtype) for array in arrays],
        in_specs=[pl.BlockSpec(memory_space=pltpu.HBM)] * len(arrays),
        out_specs=[pl.BlockSpec(memory_space=pltpu.VMEM)] * len(arrays),
        scratch_shapes=[pltpu.SemaphoreType.DMA((len(arrays),))],
        compiler_params=pltpu.CompilerParams(vmem_limit_bytes=1024 * 1024),
        cost_estimate=pl.CostEstimate(
            flops=0, bytes_accessed=4 * sum(array.size for array in arrays), transcendentals=0
        ),
        name="hold_weights",
    )(*[pltpu.with_memory_space_constraint(array, pltpu.HBM) for array in arrays])


def assemble_kernel(plan, *refs):
    flag_ref, refs = refs[0], refs[1:]
    outs = refs[sum(len(places) for pieces in plan for _, _, places in pieces) :]
    at = 0
    for out_ref, pieces in zip(outs, plan):
        first = 0
        for size, pick, places in pieces:
            held = [refs[at + index][...] for index in range(len(places))]
            at += len(places)
            if pick:
                value = jnp.where(flag_ref[0] == 1, held[0], held[1])
            else:
                value = held[0]
                if len(held) > 1:
                    value = value.astype(jnp.float32)
                    for term in held[1:]:
                        value = value + term.astype(jnp.float32)
            out_ref[first : first + size] = value.astype(out_ref.dtype)
            first += size


def assemble(flag, *outputs):
    width = outputs[0][0][2][0][0].shape[1]
    wide = width // 2
    operands, specs = [], []

    def block(row):
        return lambda j: (row, j)

    for pieces in outputs:
        for size, _, terms in pieces:
            for array, first in terms:
                operands.append(array)
                specs.append(pl.BlockSpec((size, wide), block(first // size)))
    rows = [sum(size for size, _, _ in pieces) for pieces in outputs]
    return pl.pallas_call(
        functools.partial(assemble_kernel, outputs_plan(outputs)),
        grid=(2,),
        out_shape=[jax.ShapeDtypeStruct((count, width), jnp.bfloat16) for count in rows],
        in_specs=[pl.BlockSpec(memory_space=pltpu.SMEM)] + specs,
        out_specs=[pl.BlockSpec((count, wide), lambda j: (0, j)) for count in rows],
        compiler_params=pltpu.CompilerParams(vmem_limit_bytes=12 * 1024 * 1024),
        cost_estimate=pl.CostEstimate(
            flops=2 * sum(rows) * width, bytes_accessed=8 * sum(rows) * width, transcendentals=0
        ),
        name="assemble",
    )(flag, *operands)


def outputs_plan(outputs):
    return [[(size, pick, [None] * len(terms)) for size, pick, terms in out] for out in outputs]


def experts_dense(resid, normed, weights, member, gate_weight, up_weight, down_weight, score_weight):
    f32 = jnp.float32
    n = normed.shape[0]
    h = n // 2
    z = lax.axis_index("exp") // GRID[0]
    middle = ((z == 1) | (z == 2)).astype(jnp.int32)[None]
    rest = jnp.dot(down_weight[0].astype(f32), score_weight, precision=lax.Precision.HIGHEST)
    terms = []
    for _ in range(3):
        terms.append(rest.astype(jnp.bfloat16))
        rest = rest - terms[-1].astype(f32)
    relevance = jnp.pad(jnp.stack(terms), ((0, 13), (0, 0)))
    calls = {
        "0": [(0, i) for i in range(4)],
        "p": [(1, i) for i in range(3)],
        "q": [(2, i) for i in range(3)],
        "r": [(3, i) for i in range(3)],
        "e": [(3, 3), (2, 3), (1, 3)],
    }
    order = [
        (name, slot, side, i)
        for name, blocks in calls.items()
        for side in (1, 0)
        for slot, i in blocks
    ]
    own_score = jnp.dot(resid.astype(f32), score_weight, precision=lax.Precision.HIGHEST)
    by_slot = weights.transpose(3, 4, 0, 1, 2, 5).reshape(4, 2, 4, n)
    scale = jnp.stack([by_slot[slot, side, i] for _, slot, side, i in order])
    own_sums = jnp.sum(member[0, 0, 0, 0, 0] * own_score[None], axis=1)
    experts = (gate_weight, up_weight, down_weight)
    normed, scale, member, relevance = together(normed, scale, member, relevance)

    def join(*blocks):
        return jnp.concatenate(blocks, axis=0)

    def work(held, name, *rows, side=1):
        first = [entry[0] for entry in order].index(name) + (1 - side) * len(calls[name])
        return weighted_pieces(rows, scale, first, relevance, held or experts, bool(held))

    def swap(rows):
        return move(rows, over_core)

    def keep(size, array, first=0):
        return (size, False, [(array, first)])

    p, m = move(normed, z_pair), move(normed, z_middle)
    x0, y0 = move(normed, over_x), move(normed, over_y)
    p, m, x0, y0, experts = together(p, m, x0, y0, experts)
    held = hold(*experts)

    to_x, to_y = assemble(
        middle, [keep(n, p), keep(h, y0, h)], [keep(n, p), keep(h, x0)]
    )
    px, py = move(to_x, over_x), move(to_y, over_y)
    q_middle, q_end = move(p, z_middle), move(m, z_outward)
    px, py, q_middle, q_end, held = together(px, py, q_middle, q_end, held)

    (q,) = assemble(middle, [(n, True, [(q_middle, 0), (q_end, 0)])])
    qx, qy = move(q, over_x), move(q, over_y)
    r_end = move(q, z_outward)
    d0 = join(py[n:], px[n:])
    rows_0 = join(normed, x0, y0, d0)
    out_0 = work(held, "0", swap(rows_0), rows_0)
    qx, qy, r_end, out_0 = together(qx, qy, r_end, out_0)

    pick = (n, True, [(m, 0), (r_end, 0)])
    to_x, to_y, r = assemble(middle, [pick, keep(h, qy, h)], [pick, keep(h, qx)], [pick])
    rx, ry = move(to_x, over_x), move(to_y, over_y)
    dp = move(d0, z_pair)
    rows_p = join(p, px[:n], py[:n])
    rows_q = join(q, qx, qy)
    other_q = swap(rows_q)
    out_p = work(held, "p", swap(rows_p), rows_p)
    out_q = work(held, "q", other_q, rows_q)
    rx, ry, dp, out_p, out_q = together(rx, ry, dp, out_p, out_q)

    by_x, by_y = move(ry[h:n], over_x), move(rx[:h], over_y)
    rows_r = join(r, rx[:n], ry[:n])
    other_r, came_p = swap(rows_r), swap(out_p[0])
    mine_r = work(held, "r", rows_r, side=0)
    by_x, by_y, other_r, mine_r, came_p, out_0, out_q = together(
        by_x, by_y, other_r, mine_r, came_p, out_0, out_q
    )

    rows_e = join(by_y, by_x, ry[n:], rx[n:], dp)
    other_e = swap(rows_e)
    def far(array):
        return pltpu.with_memory_space_constraint(array, pltpu.HBM)

    def both(size, out, came, first, *more):
        return (size, False, [(far(out[1]), first), (far(came), first), *more])

    def of_x(out, came, more):
        return [both(h, out, came, n, more), both(h, out, came, n + h)]

    def of_y(out, came, more):
        return [both(h, out, came, 2 * n), both(h, out, came, 2 * n + h, more)]

    def own(out, came, *more):
        return [both(n, out, came, 0, *[(array, 0) for array in more])]

    to_x, to_y = assemble(middle, [both(n, out_p, came_p, n)], [both(n, out_p, came_p, 2 * n)])
    px, py = move(to_x, over_x), move(to_y, over_y)
    came_0 = swap(out_0[0])
    out_e = work(held, "e", other_e, rows_e)
    came_e = swap(out_e[0])
    other_r, out_e, px, py = together(other_r, out_e, px, py)
    theirs_r = work(held, "r", other_r, side=1)
    out_r = (theirs_r[0], mine_r[0], jnp.concatenate([theirs_r[1], mine_r[1]], axis=0))
    came_r = swap(theirs_r[0])
    to_y, to_x = assemble(middle, [both(h, out_e, came_e, 0)], [both(h, out_e, came_e, h)])
    from_y, from_x = move(to_y, over_y), move(to_x, over_x)
    outs = {"0": out_0, "p": out_p, "q": out_q, "r": out_r, "e": out_e}
    rows = join(*[outs[name][2] for name in calls])
    from_y, from_x, came_0, came_r, out_q, rows = together(
        from_y, from_x, came_0, came_r, out_q, rows
    )
    found = {(slot, side, i): at for at, (_, slot, side, i) in enumerate(order)}
    scores = jnp.stack(
        [rows[found[slot, side, i]] for side in (0, 1) for i in range(4) for slot in range(4)]
    ).reshape(2, 2, 2, 2, 2, n)
    doc_sums = jnp.sum(member * scores[..., None, :], axis=(2, 3, 4, 6))
    doc_sums = doc_sums.at[0, 0].add(own_sums)
    req = lax.axis_index("req")
    doc_sums = jnp.where(req % 2 == 1, doc_sums[::-1], doc_sums)
    doc_sums = jnp.where(req // 2 == 1, doc_sums[:, ::-1], doc_sums)
    doc_sums = jnp.broadcast_to(
        doc_sums.transpose(1, 0, 2)[:, :, None], (2, 2, lax.axis_size("exp"), doc_sums.shape[2])
    ).reshape(-1, doc_sums.shape[2])
    to_x, to_y, to_pair = assemble(
        middle,
        of_x(out_r, came_r, (from_y, 0)) + [both(h, out_e, came_e, n + h)],
        of_y(out_r, came_r, (from_x, 0)) + [both(h, out_e, came_e, n)],
        [both(n, out_e, came_e, 2 * n)],
    )
    rx, ry = move(to_x, over_x), move(to_y, over_y)
    d_more = move(to_pair, z_pair)
    came_q = swap(out_q[0])
    doc_sums = lax.all_to_all(doc_sums, ALL, split_axis=0, concat_axis=0, tiled=True)
    rx, ry, d_more, doc_sums, came_q = together(rx, ry, d_more, doc_sums, came_q)

    to_x, to_y, sum_r = assemble(
        middle,
        of_x(out_q, came_q, (ry, n)),
        of_y(out_q, came_q, (rx, n)),
        own(out_r, came_r, rx, ry),
    )
    qx, qy = move(to_x, over_x), move(to_y, over_y)
    q_more = move(sum_r, z_inward)
    qx, qy, q_more = together(qx, qy, q_more)

    to_x, to_y, sum_q = assemble(
        middle,
        [both(h, out_0, came_0, 3 * n + h, (d_more, h))],
        [both(h, out_0, came_0, 3 * n, (d_more, 0))],
        own(out_q, came_q, qx, qy, q_more),
    )
    d_x, d_y = move(to_x, over_x), move(to_y, over_y)
    p_more, r_more = move(sum_q, z_middle), move(sum_q, z_inward)
    d_x, d_y, p_more, r_more = together(d_x, d_y, p_more, r_more)

    to_x, to_y, sum_p, sum_r = assemble(
        middle,
        of_x(out_0, came_0, (d_y, 0)),
        of_y(out_0, came_0, (d_x, 0)),
        own(out_p, came_p, px, py, p_more),
        own(out_r, came_r, rx, ry, r_more),
    )
    x0, y0 = move(to_x, over_x), move(to_y, over_y)
    from_p, from_r = move(sum_p, z_pair), move(sum_r, z_middle)
    (layer_out,) = assemble(middle, own(out_0, came_0, x0, y0, from_p, from_r, resid))
    return layer_out, jnp.sum(doc_sums, axis=0)


def is_small():
    return (lax.axis_size("req"), lax.axis_size("exp")) == (2 * GRID[1], GRID[0] * GRID[2])


def local(
    hidden_in,
    qkv,
    q_gain,
    k_gain,
    query_pages,
    page_table,
    doc_lengths,
    doc_query,
    out_weight,
    moe_gain,
    routes,
    route_weight,
    gate_weight,
    up_weight,
    down_weight,
    score_weight,
):
    tok_count = hidden_in.shape[0]
    exp_index = lax.axis_index("exp")
    doc_len = doc_lengths[0]
    tables = start_tables(routes, route_weight) if is_small() else doc_len
    attn, tables = attention(
        qkv, q_gain, k_gain, query_pages, page_table, doc_lengths, doc_query, tables
    )
    attn = attn.transpose(1, 0, 2).reshape(hidden_in.shape)
    mixed = jnp.dot(attn, out_weight, preferred_element_type=jnp.float32)
    resid = (hidden_in.astype(jnp.float32) + mixed).astype(jnp.bfloat16)
    normed = rms_scale(resid.astype(jnp.float32), moe_gain).astype(jnp.bfloat16)
    if is_small():
        weights, member = finish_tables(tables, doc_len)
        layer_out, doc_sums = experts_dense(
            resid,
            normed,
            weights,
            member,
            gate_weight,
            up_weight,
            down_weight,
            score_weight,
        )
        return (layer_out, (doc_sums / doc_len.astype(jnp.float32))[None, :])
    combined = experts_by_slots(
        normed, routes, route_weight, gate_weight, up_weight, down_weight
    )
    layer_out = (resid.astype(jnp.float32) + combined).astype(jnp.bfloat16)
    token_score = jnp.dot(
        layer_out.astype(jnp.float32), score_weight, precision=lax.Precision.HIGHEST
    )
    doc_ends = jnp.cumsum(doc_len, dtype=jnp.int32)
    own_pos = exp_index * tok_count + jnp.arange(tok_count, dtype=jnp.int32)
    member = (own_pos[:, None] < doc_ends[None, :]) & (
        own_pos[:, None] >= (doc_ends - doc_len)[None, :]
    )
    doc_partial = jnp.dot(
        token_score, member.astype(jnp.float32), precision=lax.Precision.HIGHEST
    )
    doc_sums = lax.psum(doc_partial, "exp")
    doc_scores = (doc_sums / doc_len.astype(jnp.float32))[None, :]
    return (layer_out, doc_scores)


def solution(mesh):
    in_specs = (
        P(("req", "exp"), None),
        P(("req", "exp"), None),
        P(),
        P(),
        P("req", None, None, "exp"),
        P("req", None),
        P("req", None),
        P("req", None),
        P(),
        P(),
        P(("req", "exp"), None),
        P(("req", "exp"), None),
        P(("req", "exp"), None, None),
        P(("req", "exp"), None, None),
        P(("req", "exp"), None, None),
        P(),
    )
    out_specs = (P(("req", "exp"), None), P("req", None))
    return jax.shard_map(local, mesh=mesh, in_specs=in_specs, out_specs=out_specs, check_vma=False)
```

```python
import functools

import jax
import jax.numpy as jnp
import numpy as np
from jax import lax
from jax.experimental import pallas as pl
from jax.experimental.pallas import tpu as pltpu
from jax.sharding import PartitionSpec as P

HEADS = 16
HD = 128
TOP = 8
PAGE = 128
LANES = 128
ALL = ("req", "exp")


eps = 1e-06
rope_base = 50000.0
neg_fill = -1e30


def rms_scale(values, gain_vec):
    mean_sq = jnp.mean(values * values, axis=-1, keepdims=True)
    return values * lax.rsqrt(mean_sq + eps) * gain_vec


def rope_table():
    half_dim = HD // 2
    frequency = rope_base ** (-(np.arange(half_dim) * 2.0 / HD))
    angles = (PAGE + np.arange(PAGE))[:, None] * frequency[None, :]
    cosine, sine = np.cos(angles), np.sin(angles)
    rest = np.concatenate([cosine, cosine, -sine, sine], axis=1).astype(np.float32)
    terms = []
    for _ in range(3):
        term = rest.astype(jnp.bfloat16)
        terms.append(term)
        rest = rest - term.astype(np.float32)
    return np.concatenate(terms, axis=1)


def attention_kernel(
    qkv_ref, pages_ref, len_ref, query_ref, table_ref, q_gain_ref, k_gain_ref, rope_ref,
    out_ref, q_rows, k_rows,
):
    tokens = qkv_ref.shape[0]
    heads = qkv_ref.shape[1] // (3 * HD)
    blocks = tokens // LANES
    keys = pages_ref.shape[0]
    score_scale = HD ** (-0.5) * 1.4426950408889634

    row_ids = lax.broadcasted_iota(jnp.int32, (LANES, LANES), 0)
    lane_ids = lax.broadcasted_iota(jnp.int32, (LANES, LANES), 1)
    lane_f32 = lane_ids.astype(jnp.float32)
    upper = (row_ids <= lane_ids).astype(jnp.bfloat16)
    lens = jnp.broadcast_to(len_ref[...].astype(jnp.bfloat16), (16, LANES))
    ends = jnp.dot(lens, upper, preferred_element_type=jnp.float32)[0:1]
    slot = lax.broadcasted_iota(jnp.int32, (table_ref.shape[0], LANES), 0)
    doc_page = jnp.sum(
        jnp.where(slot == query_ref[...], table_ref[...], 0).astype(jnp.float32),
        axis=0, keepdims=True,
    )

    def places(block):
        own = (row_ids + block * LANES).astype(jnp.float32)
        passed = own >= ends
        start = jnp.max(jnp.where(passed, ends, 0.0), axis=1, keepdims=True)
        stop = jnp.min(jnp.where(passed, 1e9, ends), axis=1, keepdims=True)
        doc = jnp.sum(passed.astype(jnp.float32), axis=1, keepdims=True)
        page = jnp.sum(jnp.where(lane_f32 == doc, doc_page, 0.0), axis=1, keepdims=True)
        return own, start, stop, page

    @pl.loop(0, blocks)
    def _(block):
        rows = pl.ds(pl.multiple_of(block * LANES, LANES), LANES)
        own, start, _, _ = places(block)
        onehot = (lane_f32 == own - start).astype(jnp.bfloat16)
        terms = jnp.dot(onehot, rope_ref[...], preferred_element_type=jnp.float32)
        both = terms[:, : 2 * HD] + (terms[:, 2 * HD : 4 * HD] + terms[:, 4 * HD :])
        cosine, sine = both[:, :HD], both[:, HD:]
        for part, gain_ref, kept in ((0, q_gain_ref, q_rows), (1, k_gain_ref, k_rows)):
            for head in range(heads):
                at = (part * heads + head) * HD
                values = qkv_ref[rows, at : at + HD].astype(jnp.float32)
                values = rms_scale(values, gain_ref[...])
                swapped = pltpu.roll(values, HD // 2, 1)
                kept[rows, head * HD : (head + 1) * HD] = (
                    values * cosine + swapped * sine
                ).astype(jnp.bfloat16)

    many = 2 * LANES
    page_of_key = (
        lax.broadcasted_iota(jnp.int32, (many, keys), 1) // PAGE
    ).astype(jnp.float32)
    wide = 4 * LANES
    key_at = lax.broadcasted_iota(jnp.int32, (many, wide), 1)

    @pl.loop(0, blocks // 2)
    def _(block):
        rows = pl.ds(pl.multiple_of(block * many, many), many)
        first = pl.multiple_of(jnp.clip(2 * block - 1, 0, blocks - 4) * LANES, LANES)
        window = pl.ds(first, wide)
        upper_half, lower_half = places(2 * block), places(2 * block + 1)
        start, stop, page = (
            jnp.concatenate(pair, axis=0) for pair in zip(upper_half[1:], lower_half[1:])
        )
        position = (key_at + first).astype(jnp.float32)
        in_page = page_of_key == page
        in_doc = (position >= start) & (position < stop)
        for head in range(heads):
            cols = slice(head * HD, (head + 1) * HD)
            query = q_rows[rows, cols]
            page_keys = pages_ref[:, 2 * head * HD : (2 * head + 1) * HD]
            page_values = pages_ref[:, (2 * head + 1) * HD : (2 * head + 2) * HD]
            at = (2 * heads + head) * HD
            contract = (((1,), (1,)), ((), ()))
            far = lax.dot_general(
                query, page_keys, contract, preferred_element_type=jnp.float32
            )
            near = lax.dot_general(
                query, k_rows[window, cols], contract, preferred_element_type=jnp.float32
            )
            far = jnp.where(in_page, far, neg_fill)
            near = jnp.where(in_doc, near, neg_fill)
            top = jnp.maximum(
                jnp.max(far, axis=1, keepdims=True), jnp.max(near, axis=1, keepdims=True)
            )
            far = jnp.exp2((far - top) * score_scale)
            near = jnp.exp2((near - top) * score_scale)
            total = jnp.sum(far, axis=1, keepdims=True) + jnp.sum(near, axis=1, keepdims=True)
            weighted = jnp.dot(
                far.astype(jnp.bfloat16), page_values, preferred_element_type=jnp.float32
            ) + jnp.dot(
                near.astype(jnp.bfloat16),
                qkv_ref[window, at : at + HD],
                preferred_element_type=jnp.float32,
            )
            out_ref[rows, cols] = (weighted / total).astype(jnp.bfloat16)


def pack_kernel(exp_count, qkv_ref, out_ref):
    rows = qkv_ref.shape[0]
    own = qkv_ref.shape[1] // (3 * exp_count)
    for index in range(exp_count):
        for part in range(3):
            at = (part * exp_count + index) * own
            out_ref[index * rows : (index + 1) * rows, part * own : (part + 1) * own] = qkv_ref[
                :, at : at + own
            ]


def attention(qkv, q_gain, k_gain, pages, page_table, doc_len, doc_query, tables):
    tok_count, width = qkv.shape[0], qkv.shape[1] // 3
    exp_count = lax.axis_size("exp")
    own = width // exp_count
    tokens = exp_count * tok_count
    parts = pl.pallas_call(
        functools.partial(pack_kernel, exp_count),
        out_shape=jax.ShapeDtypeStruct((tokens, 3 * own), jnp.bfloat16),
        compiler_params=pltpu.CompilerParams(vmem_limit_bytes=8 * 1024 * 1024),
        name="pack_heads",
    )(qkv)
    group = lax.all_to_all(parts, "exp", split_axis=0, concat_axis=0, tiled=True)
    docs = doc_len.shape[1]
    spare = ((0, 0), (0, LANES - docs))
    out = pl.pallas_call(
        attention_kernel,
        out_shape=jax.ShapeDtypeStruct((tokens, own), jnp.bfloat16),
        scratch_shapes=[
            pltpu.VMEM((tokens, own), jnp.bfloat16),
            pltpu.VMEM((tokens, own), jnp.bfloat16),
        ],
        compiler_params=pltpu.CompilerParams(vmem_limit_bytes=14 * 1024 * 1024),
        name="paged_attention",
    )(
        group,
        pages.reshape(-1, 2 * own),
        jnp.pad(doc_len, spare),
        jnp.pad(doc_query, spare, constant_values=-1),
        page_table.reshape(-1, 1),
        q_gain.reshape(1, HD),
        k_gain.reshape(1, HD),
        jnp.asarray(rope_table()),
    )
    out, tables = lax.optimization_barrier((out, tables))
    back = lax.all_to_all(out, "exp", split_axis=0, concat_axis=0, tiled=True)
    return back.reshape(exp_count, tok_count, own), tables


def expert_kernel(sides, steps, first, held, *refs):
    rows_refs, refs = refs[:sides], refs[sides:]
    scale_ref, relevance_ref, *weight_refs = refs[:5]
    out_refs, score_ref = refs[5 : 5 + sides], refs[5 + sides]
    step = pl.program_id(0)
    per_tile = rows_refs[0].shape[0] // LANES
    if held:
        gate, up, down = (ref.at[0] for ref in weight_refs)
    else:
        gate, up, down, sems = refs[6 + sides :]
        copies = [
            pltpu.make_async_copy(source.at[0], target, sems.at[at])
            for at, (source, target) in enumerate(zip(weight_refs, (gate, up, down)))
        ]

    def work(rows_ref, out_ref, arriving):
        rows = rows_ref[...]
        if arriving:
            copies[0].wait()
        gate_act = jnp.dot(rows, gate[...], preferred_element_type=jnp.float32)
        if arriving:
            copies[1].wait()
        up_act = jnp.dot(rows, up[...], preferred_element_type=jnp.float32)
        spread = [
            jnp.broadcast_to(
                scale_ref[pl.ds(first + step * per_tile + part, 1)], (LANES, LANES)
            ).T
            for part in range(per_tile)
        ]
        scale = jnp.concatenate(spread, axis=0)
        scale = jnp.concatenate([scale] * (up_act.shape[1] // LANES), axis=1)
        hidden_act = (jax.nn.silu(gate_act) * (up_act * scale)).astype(jnp.bfloat16)
        score = lax.dot_general(
            relevance_ref[...], hidden_act, (((1,), (1,)), ((), ())),
            preferred_element_type=jnp.float32,
        )
        score = jnp.sum(score, axis=0, keepdims=True)
        for part in range(per_tile):
            score_ref[pl.ds(step * per_tile + part, 1)] = score[
                :, part * LANES : (part + 1) * LANES
            ]
        if arriving:
            copies[2].wait()
        out_ref[...] = jnp.dot(
            hidden_act, down[...], preferred_element_type=jnp.float32
        ).astype(jnp.bfloat16)

    if not held:

        @pl.when(step == 0)
        def _():
            for copy in copies:
                copy.start()
            work(rows_refs[0], out_refs[0], True)

    for side in range(sides):
        mine = step // steps == side
        if not held and side == 0:
            mine = mine & (step > 0)

        @pl.when(mine)
        def _():
            work(rows_refs[side], out_refs[side], False)


def weighted_pieces(rows, scale, first, relevance, weights, held):
    sides = len(rows)
    count, width = rows[0].shape
    hidden = weights[0].shape[2]
    tile = 256 if count % 256 == 0 else count
    steps = count // tile
    space = pltpu.VMEM if held else pltpu.HBM
    weights = [pltpu.with_memory_space_constraint(weight, space) for weight in weights]

    def rows_of(side):
        return pl.BlockSpec((tile, width), lambda i: (jnp.clip(i - side * steps, 0, steps - 1), 0))

    fetched = [pltpu.VMEM(weight.shape[1:], jnp.bfloat16) for weight in weights]
    kept = [jax.ShapeDtypeStruct, pltpu.HBM][-sides:]
    return pl.pallas_call(
        functools.partial(expert_kernel, sides, steps, first, held),
        grid=(sides * steps,),
        out_shape=[make((count, width), jnp.bfloat16) for make in kept]
        + [jax.ShapeDtypeStruct((sides * count // LANES, LANES), jnp.float32)],
        in_specs=[rows_of(side) for side in range(sides)]
        + [
            pl.BlockSpec(scale.shape, lambda i: (0, 0)),
            pl.BlockSpec(relevance.shape, lambda i: (0, 0)),
        ]
        + [pl.BlockSpec(memory_space=space)] * 3,
        out_specs=[rows_of(side) for side in range(sides)]
        + [pl.BlockSpec((sides * count // LANES, LANES), lambda i: (0, 0))],
        scratch_shapes=[] if held else fetched + [pltpu.SemaphoreType.DMA((3,))],
        compiler_params=pltpu.CompilerParams(
            vmem_limit_bytes=((14 if tile <= 256 else 19) + (0 if held else 7)) * 1024 * 1024
        ),
        cost_estimate=pl.CostEstimate(
            flops=6 * sides * count * width * hidden,
            bytes_accessed=4 * sides * count * width + 6 * width * hidden,
            transcendentals=sides * count * hidden,
        ),
        name="expert_half",
    )(*rows, scale, relevance, *weights)


def expert_piece(rows, gate_weight, up_weight, down_weight):
    gate_act = jnp.dot(rows, gate_weight[0], preferred_element_type=jnp.float32)
    up_act = jnp.dot(rows, up_weight[0], preferred_element_type=jnp.float32)
    hidden_act = jax.nn.silu(gate_act) * up_act
    piece_out = jnp.dot(
        hidden_act.astype(jnp.bfloat16), down_weight[0], preferred_element_type=jnp.float32
    )
    return piece_out.astype(jnp.bfloat16)


def slot_numbers(route_flat, bin_count):
    onehot = (route_flat[:, None] == jnp.arange(bin_count, dtype=jnp.int32)[None, :]).astype(
        jnp.int32
    )
    prior_count = jnp.cumsum(onehot, axis=0, dtype=jnp.int32) - onehot
    return jnp.sum(prior_count * onehot, axis=1, dtype=jnp.int32)


def experts_by_slots(normed, routes, route_weight, gate_weight, up_weight, down_weight):
    tok_count, width = normed.shape
    devices = lax.axis_size("req") * lax.axis_size("exp")
    experts = devices // 2
    capacity = 2 * max(1, 3 * tok_count * TOP // (4 * experts))
    route_flat = routes.reshape(-1)
    slots = slot_numbers(route_flat, experts)
    place = route_flat * capacity + slots
    token_ids = jnp.arange(tok_count * TOP, dtype=jnp.int32) // TOP
    slot_tokens = jnp.full((experts * capacity,), tok_count, jnp.int32).at[place].set(token_ids)
    padded_rows = jnp.concatenate([normed, jnp.zeros((1, width), jnp.bfloat16)], axis=0)
    outgoing = padded_rows[slot_tokens].reshape(experts, capacity, width)
    doubled = jnp.broadcast_to(outgoing[:, None], (experts, 2, capacity, width)).reshape(
        2 * experts, capacity, width
    )
    arrived = lax.all_to_all(doubled, ALL, split_axis=0, concat_axis=0, tiled=True)
    pieces = expert_piece(arrived.reshape(-1, width), gate_weight, up_weight, down_weight)
    returned = lax.all_to_all(
        pieces.reshape(arrived.shape), ALL, split_axis=0, concat_axis=0, tiled=True
    ).reshape(experts, 2, capacity, width)
    results = (returned[:, 0].astype(jnp.float32) + returned[:, 1].astype(jnp.float32)).astype(
        jnp.bfloat16
    )
    picked = results.reshape(experts * capacity, width)[place].reshape(tok_count, TOP, width)
    return jnp.einsum("tk,tkd->td", route_weight, picked.astype(jnp.float32))


GRID = (2, 2, 4)


def device_number(x, y, z, core):
    return ((y * 2 + core) * GRID[2] + z) * GRID[0] + x


def pairs(target):
    found = []
    for y in range(GRID[1]):
        for core in range(2):
            for z in range(GRID[2]):
                for x in range(GRID[0]):
                    to = target(x, y, z, core)
                    if to is not None:
                        found.append((device_number(x, y, z, core), device_number(*to)))
    return found


def move(block, target):
    return lax.ppermute(block, ALL, pairs(target))


def over_x(x, y, z, core):
    return (1 - x, y, z, core)


def over_y(x, y, z, core):
    return (x, 1 - y, z, core)


def over_core(x, y, z, core):
    return (x, y, z, 1 - core)


def z_pair(x, y, z, core):
    return (x, y, z ^ 1, core)


def z_far(x, y, z, core):
    return (x, y, z ^ 2, core)


def z_middle(x, y, z, core):
    return (x, y, 3 - z, core) if z in (1, 2) else None


def z_outward(x, y, z, core):
    return (x, y, {1: 0, 2: 3}[z], core) if z in (1, 2) else None


def z_inward(x, y, z, core):
    return (x, y, {0: 1, 3: 2}[z], core) if z in (0, 3) else None


def together(*values):
    return lax.optimization_barrier(values)


def start_tables(routes, route_weight):
    experts = lax.axis_size("req") * lax.axis_size("exp") // 2
    chosen = routes.T[None] == jnp.arange(experts, dtype=jnp.int32)[:, None, None]
    dense = jnp.sum(jnp.where(chosen, route_weight.T[None], 0.0), axis=1)
    for target in (z_pair, z_far):
        dense = jnp.stack([dense, move(dense, target)])
    return dense


def finish_tables(dense, doc_len):
    tok_count = dense.shape[-1]
    for target in (over_x, over_y, over_core):
        dense = jnp.stack([dense, move(dense, target)])
    exp = lax.axis_index("exp")
    own_expert = (lax.axis_index("req") * lax.axis_size("exp") + exp) // 2
    weights = lax.dynamic_index_in_dim(dense, own_expert, 5, False)
    ends = jnp.cumsum(doc_len, dtype=jnp.int32)
    bounds = jnp.stack([ends - doc_len, ends])
    for target in (over_y, over_core):
        bounds = jnp.stack([bounds, move(bounds, target)])
    flips = np.array([[[k1 * 4 + k0 * 2 + dx for k0 in (0, 1)] for k1 in (0, 1)] for dx in (0, 1)])
    blocks = jnp.bitwise_xor(exp, jnp.asarray(flips, jnp.int32))
    position = blocks[..., None] * tok_count + jnp.arange(tok_count, dtype=jnp.int32)
    position = position[None, None, ..., None, :]

    def spread(side):
        return bounds[:, :, side][:, :, None, None, None, :, None]

    return weights, ((position >= spread(0)) & (position < spread(1))).astype(jnp.float32)


def hold_kernel(*refs):
    count = (len(refs) - 1) // 2
    copies = [
        pltpu.make_async_copy(refs[at], refs[count + at], refs[-1].at[at]) for at in range(count)
    ]
    for copy in copies:
        copy.start()
    for copy in copies:
        copy.wait()


def hold(*arrays):
    return pl.pallas_call(
        hold_kernel,
        out_shape=[pltpu.VMEM(array.shape, array.dtype) for array in arrays],
        in_specs=[pl.BlockSpec(memory_space=pltpu.HBM)] * len(arrays),
        out_specs=[pl.BlockSpec(memory_space=pltpu.VMEM)] * len(arrays),
        scratch_shapes=[pltpu.SemaphoreType.DMA((len(arrays),))],
        compiler_params=pltpu.CompilerParams(vmem_limit_bytes=1024 * 1024),
        cost_estimate=pl.CostEstimate(
            flops=0, bytes_accessed=4 * sum(array.size for array in arrays), transcendentals=0
        ),
        name="hold_weights",
    )(*[pltpu.with_memory_space_constraint(array, pltpu.HBM) for array in arrays])


def assemble_kernel(plan, *refs):
    flag_ref, refs = refs[0], refs[1:]
    outs = refs[sum(len(places) for pieces in plan for _, _, places in pieces) :]
    at = 0
    for out_ref, pieces in zip(outs, plan):
        first = 0
        for size, pick, places in pieces:
            held = [refs[at + index][...] for index in range(len(places))]
            at += len(places)
            if pick:
                value = jnp.where(flag_ref[0] == 1, held[0], held[1])
            else:
                value = held[0]
                if len(held) > 1:
                    value = value.astype(jnp.float32)
                    for term in held[1:]:
                        value = value + term.astype(jnp.float32)
            out_ref[first : first + size] = value.astype(out_ref.dtype)
            first += size


def assemble(flag, *outputs, steps=2):
    width = outputs[0][0][2][0][0].shape[1]
    wide = width // steps
    operands, specs = [], []

    def block(row):
        return lambda j: (row, j)

    for pieces in outputs:
        for size, _, terms in pieces:
            for array, first in terms:
                operands.append(array)
                specs.append(pl.BlockSpec((size, wide), block(first // size)))
    rows = [sum(size for size, _, _ in pieces) for pieces in outputs]
    return pl.pallas_call(
        functools.partial(assemble_kernel, outputs_plan(outputs)),
        grid=(steps,),
        out_shape=[jax.ShapeDtypeStruct((count, width), jnp.bfloat16) for count in rows],
        in_specs=[pl.BlockSpec(memory_space=pltpu.SMEM)] + specs,
        out_specs=[pl.BlockSpec((count, wide), lambda j: (0, j)) for count in rows],
        compiler_params=pltpu.CompilerParams(vmem_limit_bytes=16 * 1024 * 1024),
        cost_estimate=pl.CostEstimate(
            flops=2 * sum(rows) * width, bytes_accessed=8 * sum(rows) * width, transcendentals=0
        ),
        name="assemble",
    )(flag, *operands)


def outputs_plan(outputs):
    return [[(size, pick, [None] * len(terms)) for size, pick, terms in out] for out in outputs]


def experts_dense(resid, normed, weights, member, gate_weight, up_weight, down_weight, score_weight):
    f32 = jnp.float32
    n = normed.shape[0]
    h = n // 2
    z = lax.axis_index("exp") // GRID[0]
    middle = ((z == 1) | (z == 2)).astype(jnp.int32)[None]
    rest = jnp.dot(down_weight[0].astype(f32), score_weight, precision=lax.Precision.HIGHEST)
    terms = []
    for _ in range(3):
        terms.append(rest.astype(jnp.bfloat16))
        rest = rest - terms[-1].astype(f32)
    relevance = jnp.pad(jnp.stack(terms), ((0, 13), (0, 0)))
    calls = {
        "0": [(0, i) for i in range(4)],
        "p": [(1, i) for i in range(3)],
        "q": [(2, i) for i in range(3)],
        "r": [(3, i) for i in range(3)],
        "e": [(3, 3), (2, 3), (1, 3)],
    }
    order = [
        (name, slot, side, i)
        for name, blocks in calls.items()
        for side in (1, 0)
        for slot, i in blocks
    ]
    own_score = jnp.dot(resid.astype(f32), score_weight, precision=lax.Precision.HIGHEST)
    by_slot = weights.transpose(3, 4, 0, 1, 2, 5).reshape(4, 2, 4, n)
    scale = jnp.stack([by_slot[slot, side, i] for _, slot, side, i in order])
    own_sums = jnp.sum(member[0, 0, 0, 0, 0] * own_score[None], axis=1)
    experts = (gate_weight, up_weight, down_weight)
    normed, scale, member, relevance = together(normed, scale, member, relevance)

    def join(*blocks):
        return jnp.concatenate(blocks, axis=0)

    def work(held, name, *rows, side=1):
        first = [entry[0] for entry in order].index(name) + (1 - side) * len(calls[name])
        return weighted_pieces(rows, scale, first, relevance, held or experts, bool(held))

    def swap(rows):
        return move(rows, over_core)

    def keep(size, array, first=0):
        return (size, False, [(array, first)])

    p, m = move(normed, z_pair), move(normed, z_middle)
    x0, y0 = move(normed, over_x), move(normed, over_y)
    p, m, x0, y0, experts = together(p, m, x0, y0, experts)
    held = hold(*experts)

    to_x, to_y = assemble(
        middle, [keep(n, p), keep(h, y0, h)], [keep(n, p), keep(h, x0)], steps=1
    )
    px, py = move(to_x, over_x), move(to_y, over_y)
    q_middle, q_end = move(p, z_middle), move(m, z_outward)
    px, py, q_middle, q_end, held = together(px, py, q_middle, q_end, held)

    (q,) = assemble(middle, [(n, True, [(q_middle, 0), (q_end, 0)])], steps=1)
    qx, qy = move(q, over_x), move(q, over_y)
    r_end = move(q, z_outward)
    d0 = join(py[n:], px[n:])
    rows_0 = join(normed, x0, y0, d0)
    out_0 = work(held, "0", swap(rows_0), rows_0)
    qx, qy, r_end, out_0 = together(qx, qy, r_end, out_0)

    pick = (n, True, [(m, 0), (r_end, 0)])
    to_x, to_y, r = assemble(
        middle, [pick, keep(h, qy, h)], [pick, keep(h, qx)], [pick], steps=1
    )
    rx, ry = move(to_x, over_x), move(to_y, over_y)
    dp = move(d0, z_pair)
    rows_p = join(p, px[:n], py[:n])
    rows_q = join(q, qx, qy)
    other_q = swap(rows_q)
    out_p = work(held, "p", swap(rows_p), rows_p)
    out_q = work(held, "q", other_q, rows_q)
    rx, ry, dp, out_p, out_q = together(rx, ry, dp, out_p, out_q)

    by_x, by_y = move(ry[h:n], over_x), move(rx[:h], over_y)
    rows_r = join(r, rx[:n], ry[:n])
    other_r, came_p = swap(rows_r), swap(out_p[0])
    mine_r = work(held, "r", rows_r, side=0)
    by_x, by_y, other_r, mine_r, came_p, out_0, out_q = together(
        by_x, by_y, other_r, mine_r, came_p, out_0, out_q
    )

    rows_e = join(by_y, by_x, ry[n:], rx[n:], dp)
    other_e = swap(rows_e)
    def far(array):
        return pltpu.with_memory_space_constraint(array, pltpu.HBM)

    def both(size, out, came, first, *more):
        return (size, False, [(far(out[1]), first), (far(came), first), *more])

    def of_x(out, came, more):
        return [both(h, out, came, n, more), both(h, out, came, n + h)]

    def of_y(out, came, more):
        return [both(h, out, came, 2 * n), both(h, out, came, 2 * n + h, more)]

    def own(out, came, *more):
        return [both(n, out, came, 0, *[(array, 0) for array in more])]

    to_x, to_y = assemble(middle, [both(n, out_p, came_p, n)], [both(n, out_p, came_p, 2 * n)])
    px, py = move(to_x, over_x), move(to_y, over_y)
    came_0 = swap(out_0[0])
    out_e = work(held, "e", other_e, rows_e)
    came_e = swap(out_e[0])
    other_r, out_e, px, py = together(other_r, out_e, px, py)
    theirs_r = work(held, "r", other_r, side=1)
    out_r = (theirs_r[0], mine_r[0], jnp.concatenate([theirs_r[1], mine_r[1]], axis=0))
    came_r = swap(theirs_r[0])
    to_y, to_x = assemble(middle, [both(h, out_e, came_e, 0)], [both(h, out_e, came_e, h)])
    from_y, from_x = move(to_y, over_y), move(to_x, over_x)
    outs = {"0": out_0, "p": out_p, "q": out_q, "r": out_r, "e": out_e}
    rows = join(*[outs[name][2] for name in calls])
    from_y, from_x, came_0, came_r, out_q, rows = together(
        from_y, from_x, came_0, came_r, out_q, rows
    )
    found = {(slot, side, i): at for at, (_, slot, side, i) in enumerate(order)}
    scores = jnp.stack(
        [rows[found[slot, side, i]] for side in (0, 1) for i in range(4) for slot in range(4)]
    ).reshape(2, 2, 2, 2, 2, n)
    doc_sums = jnp.sum(member * scores[..., None, :], axis=(2, 3, 4, 6))
    doc_sums = doc_sums.at[0, 0].add(own_sums)
    req = lax.axis_index("req")
    doc_sums = jnp.where(req % 2 == 1, doc_sums[::-1], doc_sums)
    doc_sums = jnp.where(req // 2 == 1, doc_sums[:, ::-1], doc_sums)
    doc_sums = jnp.broadcast_to(
        doc_sums.transpose(1, 0, 2)[:, :, None], (2, 2, lax.axis_size("exp"), doc_sums.shape[2])
    ).reshape(-1, doc_sums.shape[2])
    to_x, to_y, to_pair = assemble(
        middle,
        of_x(out_r, came_r, (from_y, 0)) + [both(h, out_e, came_e, n + h)],
        of_y(out_r, came_r, (from_x, 0)) + [both(h, out_e, came_e, n)],
        [both(n, out_e, came_e, 2 * n)],
    )
    rx, ry = move(to_x, over_x), move(to_y, over_y)
    d_more = move(to_pair, z_pair)
    came_q = swap(out_q[0])
    doc_sums = lax.all_to_all(doc_sums, ALL, split_axis=0, concat_axis=0, tiled=True)
    rx, ry, d_more, doc_sums, came_q = together(rx, ry, d_more, doc_sums, came_q)

    to_x, to_y, sum_r = assemble(
        middle,
        of_x(out_q, came_q, (ry, n)),
        of_y(out_q, came_q, (rx, n)),
        own(out_r, came_r, rx, ry),
    )
    qx, qy = move(to_x, over_x), move(to_y, over_y)
    q_more = move(sum_r, z_inward)
    qx, qy, q_more = together(qx, qy, q_more)

    to_x, to_y, sum_q = assemble(
        middle,
        [both(h, out_0, came_0, 3 * n + h, (d_more, h))],
        [both(h, out_0, came_0, 3 * n, (d_more, 0))],
        own(out_q, came_q, qx, qy, q_more),
    )
    d_x, d_y = move(to_x, over_x), move(to_y, over_y)
    p_more, r_more = move(sum_q, z_middle), move(sum_q, z_inward)
    d_x, d_y, p_more, r_more = together(d_x, d_y, p_more, r_more)

    to_x, to_y, sum_p, sum_r = assemble(
        middle,
        of_x(out_0, came_0, (d_y, 0)),
        of_y(out_0, came_0, (d_x, 0)),
        own(out_p, came_p, px, py, p_more),
        own(out_r, came_r, rx, ry, r_more),
    )
    x0, y0 = move(to_x, over_x), move(to_y, over_y)
    from_p, from_r = move(sum_p, z_pair), move(sum_r, z_middle)
    (layer_out,) = assemble(middle, own(out_0, came_0, x0, y0, from_p, from_r, resid))
    return layer_out, jnp.sum(doc_sums, axis=0)


def is_small():
    return (lax.axis_size("req"), lax.axis_size("exp")) == (2 * GRID[1], GRID[0] * GRID[2])


def local(
    hidden_in,
    qkv,
    q_gain,
    k_gain,
    query_pages,
    page_table,
    doc_lengths,
    doc_query,
    out_weight,
    moe_gain,
    routes,
    route_weight,
    gate_weight,
    up_weight,
    down_weight,
    score_weight,
):
    tok_count = hidden_in.shape[0]
    exp_index = lax.axis_index("exp")
    doc_len = doc_lengths[0]
    tables = start_tables(routes, route_weight) if is_small() else doc_len
    attn, tables = attention(
        qkv, q_gain, k_gain, query_pages, page_table, doc_lengths, doc_query, tables
    )
    attn = attn.transpose(1, 0, 2).reshape(hidden_in.shape)
    mixed = jnp.dot(attn, out_weight, preferred_element_type=jnp.float32)
    resid = (hidden_in.astype(jnp.float32) + mixed).astype(jnp.bfloat16)
    normed = rms_scale(resid.astype(jnp.float32), moe_gain).astype(jnp.bfloat16)
    if is_small():
        weights, member = finish_tables(tables, doc_len)
        layer_out, doc_sums = experts_dense(
            resid,
            normed,
            weights,
            member,
            gate_weight,
            up_weight,
            down_weight,
            score_weight,
        )
        return (layer_out, (doc_sums / doc_len.astype(jnp.float32))[None, :])
    combined = experts_by_slots(
        normed, routes, route_weight, gate_weight, up_weight, down_weight
    )
    layer_out = (resid.astype(jnp.float32) + combined).astype(jnp.bfloat16)
    token_score = jnp.dot(
        layer_out.astype(jnp.float32), score_weight, precision=lax.Precision.HIGHEST
    )
    doc_ends = jnp.cumsum(doc_len, dtype=jnp.int32)
    own_pos = exp_index * tok_count + jnp.arange(tok_count, dtype=jnp.int32)
    member = (own_pos[:, None] < doc_ends[None, :]) & (
        own_pos[:, None] >= (doc_ends - doc_len)[None, :]
    )
    doc_partial = jnp.dot(
        token_score, member.astype(jnp.float32), precision=lax.Precision.HIGHEST
    )
    doc_sums = lax.psum(doc_partial, "exp")
    doc_scores = (doc_sums / doc_len.astype(jnp.float32))[None, :]
    return (layer_out, doc_scores)


def solution(mesh):
    in_specs = (
        P(("req", "exp"), None),
        P(("req", "exp"), None),
        P(),
        P(),
        P("req", None, None, "exp"),
        P("req", None),
        P("req", None),
        P("req", None),
        P(),
        P(),
        P(("req", "exp"), None),
        P(("req", "exp"), None),
        P(("req", "exp"), None, None),
        P(("req", "exp"), None, None),
        P(("req", "exp"), None, None),
        P(),
    )
    out_specs = (P(("req", "exp"), None), P("req", None))
    return jax.shard_map(local, mesh=mesh, in_specs=in_specs, out_specs=out_specs, check_vma=False)
```

```python
import functools

import jax
import jax.numpy as jnp
import numpy as np
from jax import lax
from jax.experimental import pallas as pl
from jax.experimental.pallas import tpu as pltpu
from jax.sharding import PartitionSpec as P

HEADS = 16
HD = 128
TOP = 8
PAGE = 128
LANES = 128
ALL = ("req", "exp")


eps = 1e-06
rope_base = 50000.0
neg_fill = -1e30


def rms_scale(values, gain_vec):
    mean_sq = jnp.mean(values * values, axis=-1, keepdims=True)
    return values * lax.rsqrt(mean_sq + eps) * gain_vec


def rope_table():
    half_dim = HD // 2
    frequency = rope_base ** (-(np.arange(half_dim) * 2.0 / HD))
    angles = (PAGE + np.arange(PAGE))[:, None] * frequency[None, :]
    cosine, sine = np.cos(angles), np.sin(angles)
    rest = np.concatenate([cosine, cosine, -sine, sine], axis=1).astype(np.float32)
    terms = []
    for _ in range(3):
        term = rest.astype(jnp.bfloat16)
        terms.append(term)
        rest = rest - term.astype(np.float32)
    return np.concatenate(terms, axis=1)


def attention_kernel(
    qkv_ref, pages_ref, len_ref, query_ref, table_ref, q_gain_ref, k_gain_ref, rope_ref,
    out_ref, q_rows, k_rows,
):
    tokens = qkv_ref.shape[0]
    heads = qkv_ref.shape[1] // (3 * HD)
    blocks = tokens // LANES
    keys = pages_ref.shape[0]
    score_scale = HD ** (-0.5) * 1.4426950408889634

    row_ids = lax.broadcasted_iota(jnp.int32, (LANES, LANES), 0)
    lane_ids = lax.broadcasted_iota(jnp.int32, (LANES, LANES), 1)
    lane_f32 = lane_ids.astype(jnp.float32)
    upper = (row_ids <= lane_ids).astype(jnp.bfloat16)
    lens = jnp.broadcast_to(len_ref[...].astype(jnp.bfloat16), (16, LANES))
    ends = jnp.dot(lens, upper, preferred_element_type=jnp.float32)[0:1]
    slot = lax.broadcasted_iota(jnp.int32, (table_ref.shape[0], LANES), 0)
    doc_page = jnp.sum(
        jnp.where(slot == query_ref[...], table_ref[...], 0).astype(jnp.float32),
        axis=0, keepdims=True,
    )

    def places(block):
        own = (row_ids + block * LANES).astype(jnp.float32)
        passed = own >= ends
        start = jnp.max(jnp.where(passed, ends, 0.0), axis=1, keepdims=True)
        stop = jnp.min(jnp.where(passed, 1e9, ends), axis=1, keepdims=True)
        doc = jnp.sum(passed.astype(jnp.float32), axis=1, keepdims=True)
        page = jnp.sum(jnp.where(lane_f32 == doc, doc_page, 0.0), axis=1, keepdims=True)
        return own, start, stop, page

    @pl.loop(0, blocks)
    def _(block):
        rows = pl.ds(pl.multiple_of(block * LANES, LANES), LANES)
        own, start, _, _ = places(block)
        onehot = (lane_f32 == own - start).astype(jnp.bfloat16)
        terms = jnp.dot(onehot, rope_ref[...], preferred_element_type=jnp.float32)
        both = terms[:, : 2 * HD] + (terms[:, 2 * HD : 4 * HD] + terms[:, 4 * HD :])
        cosine, sine = both[:, :HD], both[:, HD:]
        for part, gain_ref, kept in ((0, q_gain_ref, q_rows), (1, k_gain_ref, k_rows)):
            for head in range(heads):
                at = (part * heads + head) * HD
                values = qkv_ref[rows, at : at + HD].astype(jnp.float32)
                values = rms_scale(values, gain_ref[...])
                swapped = pltpu.roll(values, HD // 2, 1)
                kept[rows, head * HD : (head + 1) * HD] = (
                    values * cosine + swapped * sine
                ).astype(jnp.bfloat16)

    many = 2 * LANES
    page_of_key = (
        lax.broadcasted_iota(jnp.int32, (many, keys), 1) // PAGE
    ).astype(jnp.float32)
    wide = 4 * LANES
    key_at = lax.broadcasted_iota(jnp.int32, (many, wide), 1)

    @pl.loop(0, blocks // 2, unroll=4)
    def _(block):
        rows = pl.ds(pl.multiple_of(block * many, many), many)
        first = pl.multiple_of(jnp.clip(2 * block - 1, 0, blocks - 4) * LANES, LANES)
        window = pl.ds(first, wide)
        upper_half, lower_half = places(2 * block), places(2 * block + 1)
        start, stop, page = (
            jnp.concatenate(pair, axis=0) for pair in zip(upper_half[1:], lower_half[1:])
        )
        position = (key_at + first).astype(jnp.float32)
        in_page = page_of_key == page
        in_doc = (position >= start) & (position < stop)
        for head in range(heads):
            cols = slice(head * HD, (head + 1) * HD)
            query = q_rows[rows, cols]
            page_keys = pages_ref[:, 2 * head * HD : (2 * head + 1) * HD]
            page_values = pages_ref[:, (2 * head + 1) * HD : (2 * head + 2) * HD]
            at = (2 * heads + head) * HD
            contract = (((1,), (1,)), ((), ()))
            far = lax.dot_general(
                query, page_keys, contract, preferred_element_type=jnp.float32
            )
            near = lax.dot_general(
                query, k_rows[window, cols], contract, preferred_element_type=jnp.float32
            )
            far = jnp.where(in_page, far, neg_fill)
            near = jnp.where(in_doc, near, neg_fill)
            top = jnp.maximum(
                jnp.max(far, axis=1, keepdims=True), jnp.max(near, axis=1, keepdims=True)
            )
            far = jnp.exp2((far - top) * score_scale)
            near = jnp.exp2((near - top) * score_scale)
            total = jnp.sum(far, axis=1, keepdims=True) + jnp.sum(near, axis=1, keepdims=True)
            weighted = jnp.dot(
                far.astype(jnp.bfloat16), page_values, preferred_element_type=jnp.float32
            ) + jnp.dot(
                near.astype(jnp.bfloat16),
                qkv_ref[window, at : at + HD],
                preferred_element_type=jnp.float32,
            )
            out_ref[rows, cols] = (weighted / total).astype(jnp.bfloat16)


def pack_kernel(exp_count, qkv_ref, out_ref):
    rows = qkv_ref.shape[0]
    own = qkv_ref.shape[1] // (3 * exp_count)
    for index in range(exp_count):
        for part in range(3):
            at = (part * exp_count + index) * own
            out_ref[index * rows : (index + 1) * rows, part * own : (part + 1) * own] = qkv_ref[
                :, at : at + own
            ]


def attention(qkv, q_gain, k_gain, pages, page_table, doc_len, doc_query, tables):
    tok_count, width = qkv.shape[0], qkv.shape[1] // 3
    exp_count = lax.axis_size("exp")
    own = width // exp_count
    tokens = exp_count * tok_count
    parts = pl.pallas_call(
        functools.partial(pack_kernel, exp_count),
        out_shape=jax.ShapeDtypeStruct((tokens, 3 * own), jnp.bfloat16),
        compiler_params=pltpu.CompilerParams(vmem_limit_bytes=8 * 1024 * 1024),
        name="pack_heads",
    )(qkv)
    group = lax.all_to_all(parts, "exp", split_axis=0, concat_axis=0, tiled=True)
    docs = doc_len.shape[1]
    spare = ((0, 0), (0, LANES - docs))
    out = pl.pallas_call(
        attention_kernel,
        out_shape=jax.ShapeDtypeStruct((tokens, own), jnp.bfloat16),
        scratch_shapes=[
            pltpu.VMEM((tokens, own), jnp.bfloat16),
            pltpu.VMEM((tokens, own), jnp.bfloat16),
        ],
        compiler_params=pltpu.CompilerParams(vmem_limit_bytes=14 * 1024 * 1024),
        name="paged_attention",
    )(
        group,
        pages.reshape(-1, 2 * own),
        jnp.pad(doc_len, spare),
        jnp.pad(doc_query, spare, constant_values=-1),
        page_table.reshape(-1, 1),
        q_gain.reshape(1, HD),
        k_gain.reshape(1, HD),
        jnp.asarray(rope_table()),
    )
    out, tables = lax.optimization_barrier((out, tables))
    back = lax.all_to_all(out, "exp", split_axis=0, concat_axis=0, tiled=True)
    return back.reshape(exp_count, tok_count, own), tables


def expert_kernel(sides, steps, first, held, *refs):
    rows_refs, refs = refs[:sides], refs[sides:]
    scale_ref, relevance_ref, *weight_refs = refs[:5]
    out_refs, score_ref = refs[5 : 5 + sides], refs[5 + sides]
    step = pl.program_id(0)
    per_tile = rows_refs[0].shape[0] // LANES
    if held:
        gate, up, down = (ref.at[0] for ref in weight_refs)
    else:
        gate, up, down, sems = refs[6 + sides :]
        copies = [
            pltpu.make_async_copy(source.at[0], target, sems.at[at])
            for at, (source, target) in enumerate(zip(weight_refs, (gate, up, down)))
        ]

    def work(rows_ref, out_ref, arriving):
        rows = rows_ref[...]
        if arriving:
            copies[0].wait()
        gate_act = jnp.dot(rows, gate[...], preferred_element_type=jnp.float32)
        if arriving:
            copies[1].wait()
        up_act = jnp.dot(rows, up[...], preferred_element_type=jnp.float32)
        spread = [
            jnp.broadcast_to(
                scale_ref[pl.ds(first + step * per_tile + part, 1)], (LANES, LANES)
            ).T
            for part in range(per_tile)
        ]
        scale = jnp.concatenate(spread, axis=0)
        scale = jnp.concatenate([scale] * (up_act.shape[1] // LANES), axis=1)
        hidden_act = (jax.nn.silu(gate_act) * (up_act * scale)).astype(jnp.bfloat16)
        score = lax.dot_general(
            relevance_ref[...], hidden_act, (((1,), (1,)), ((), ())),
            preferred_element_type=jnp.float32,
        )
        score = jnp.sum(score, axis=0, keepdims=True)
        for part in range(per_tile):
            score_ref[pl.ds(step * per_tile + part, 1)] = score[
                :, part * LANES : (part + 1) * LANES
            ]
        if arriving:
            copies[2].wait()
        out_ref[...] = jnp.dot(
            hidden_act, down[...], preferred_element_type=jnp.float32
        ).astype(jnp.bfloat16)

    if not held:

        @pl.when(step == 0)
        def _():
            for copy in copies:
                copy.start()
            work(rows_refs[0], out_refs[0], True)

    for side in range(sides):
        mine = step // steps == side
        if not held and side == 0:
            mine = mine & (step > 0)

        @pl.when(mine)
        def _():
            work(rows_refs[side], out_refs[side], False)


def weighted_pieces(rows, scale, first, relevance, weights, held):
    sides = len(rows)
    count, width = rows[0].shape
    hidden = weights[0].shape[2]
    tile = 256 if count % 256 == 0 else count
    steps = count // tile
    space = pltpu.VMEM if held else pltpu.HBM
    weights = [pltpu.with_memory_space_constraint(weight, space) for weight in weights]

    def rows_of(side):
        return pl.BlockSpec((tile, width), lambda i: (jnp.clip(i - side * steps, 0, steps - 1), 0))

    fetched = [pltpu.VMEM(weight.shape[1:], jnp.bfloat16) for weight in weights]
    kept = [jax.ShapeDtypeStruct, pltpu.HBM][-sides:]
    return pl.pallas_call(
        functools.partial(expert_kernel, sides, steps, first, held),
        grid=(sides * steps,),
        out_shape=[make((count, width), jnp.bfloat16) for make in kept]
        + [jax.ShapeDtypeStruct((sides * count // LANES, LANES), jnp.float32)],
        in_specs=[rows_of(side) for side in range(sides)]
        + [
            pl.BlockSpec(scale.shape, lambda i: (0, 0)),
            pl.BlockSpec(relevance.shape, lambda i: (0, 0)),
        ]
        + [pl.BlockSpec(memory_space=space)] * 3,
        out_specs=[rows_of(side) for side in range(sides)]
        + [pl.BlockSpec((sides * count // LANES, LANES), lambda i: (0, 0))],
        scratch_shapes=[] if held else fetched + [pltpu.SemaphoreType.DMA((3,))],
        compiler_params=pltpu.CompilerParams(
            vmem_limit_bytes=((14 if tile <= 256 else 19) + (0 if held else 7)) * 1024 * 1024
        ),
        cost_estimate=pl.CostEstimate(
            flops=6 * sides * count * width * hidden,
            bytes_accessed=4 * sides * count * width + 6 * width * hidden,
            transcendentals=sides * count * hidden,
        ),
        name="expert_half",
    )(*rows, scale, relevance, *weights)


def expert_piece(rows, gate_weight, up_weight, down_weight):
    gate_act = jnp.dot(rows, gate_weight[0], preferred_element_type=jnp.float32)
    up_act = jnp.dot(rows, up_weight[0], preferred_element_type=jnp.float32)
    hidden_act = jax.nn.silu(gate_act) * up_act
    piece_out = jnp.dot(
        hidden_act.astype(jnp.bfloat16), down_weight[0], preferred_element_type=jnp.float32
    )
    return piece_out.astype(jnp.bfloat16)


def slot_numbers(route_flat, bin_count):
    onehot = (route_flat[:, None] == jnp.arange(bin_count, dtype=jnp.int32)[None, :]).astype(
        jnp.int32
    )
    prior_count = jnp.cumsum(onehot, axis=0, dtype=jnp.int32) - onehot
    return jnp.sum(prior_count * onehot, axis=1, dtype=jnp.int32)


def experts_by_slots(normed, routes, route_weight, gate_weight, up_weight, down_weight):
    tok_count, width = normed.shape
    devices = lax.axis_size("req") * lax.axis_size("exp")
    experts = devices // 2
    capacity = 2 * max(1, 3 * tok_count * TOP // (4 * experts))
    route_flat = routes.reshape(-1)
    slots = slot_numbers(route_flat, experts)
    place = route_flat * capacity + slots
    token_ids = jnp.arange(tok_count * TOP, dtype=jnp.int32) // TOP
    slot_tokens = jnp.full((experts * capacity,), tok_count, jnp.int32).at[place].set(token_ids)
    padded_rows = jnp.concatenate([normed, jnp.zeros((1, width), jnp.bfloat16)], axis=0)
    outgoing = padded_rows[slot_tokens].reshape(experts, capacity, width)
    doubled = jnp.broadcast_to(outgoing[:, None], (experts, 2, capacity, width)).reshape(
        2 * experts, capacity, width
    )
    arrived = lax.all_to_all(doubled, ALL, split_axis=0, concat_axis=0, tiled=True)
    pieces = expert_piece(arrived.reshape(-1, width), gate_weight, up_weight, down_weight)
    returned = lax.all_to_all(
        pieces.reshape(arrived.shape), ALL, split_axis=0, concat_axis=0, tiled=True
    ).reshape(experts, 2, capacity, width)
    results = (returned[:, 0].astype(jnp.float32) + returned[:, 1].astype(jnp.float32)).astype(
        jnp.bfloat16
    )
    picked = results.reshape(experts * capacity, width)[place].reshape(tok_count, TOP, width)
    return jnp.einsum("tk,tkd->td", route_weight, picked.astype(jnp.float32))


GRID = (2, 2, 4)


def device_number(x, y, z, core):
    return ((y * 2 + core) * GRID[2] + z) * GRID[0] + x


def pairs(target):
    found = []
    for y in range(GRID[1]):
        for core in range(2):
            for z in range(GRID[2]):
                for x in range(GRID[0]):
                    to = target(x, y, z, core)
                    if to is not None:
                        found.append((device_number(x, y, z, core), device_number(*to)))
    return found


def move(block, target):
    return lax.ppermute(block, ALL, pairs(target))


def over_x(x, y, z, core):
    return (1 - x, y, z, core)


def over_y(x, y, z, core):
    return (x, 1 - y, z, core)


def over_core(x, y, z, core):
    return (x, y, z, 1 - core)


def z_pair(x, y, z, core):
    return (x, y, z ^ 1, core)


def z_far(x, y, z, core):
    return (x, y, z ^ 2, core)


def z_middle(x, y, z, core):
    return (x, y, 3 - z, core) if z in (1, 2) else None


def z_outward(x, y, z, core):
    return (x, y, {1: 0, 2: 3}[z], core) if z in (1, 2) else None


def z_inward(x, y, z, core):
    return (x, y, {0: 1, 3: 2}[z], core) if z in (0, 3) else None


def together(*values):
    return lax.optimization_barrier(values)


def start_tables(routes, route_weight):
    experts = lax.axis_size("req") * lax.axis_size("exp") // 2
    chosen = routes.T[None] == jnp.arange(experts, dtype=jnp.int32)[:, None, None]
    dense = jnp.sum(jnp.where(chosen, route_weight.T[None], 0.0), axis=1)
    for target in (z_pair, z_far):
        dense = jnp.stack([dense, move(dense, target)])
    return dense


def finish_tables(dense, doc_len):
    tok_count = dense.shape[-1]
    for target in (over_x, over_y, over_core):
        dense = jnp.stack([dense, move(dense, target)])
    exp = lax.axis_index("exp")
    own_expert = (lax.axis_index("req") * lax.axis_size("exp") + exp) // 2
    weights = lax.dynamic_index_in_dim(dense, own_expert, 5, False)
    ends = jnp.cumsum(doc_len, dtype=jnp.int32)
    bounds = jnp.stack([ends - doc_len, ends])
    for target in (over_y, over_core):
        bounds = jnp.stack([bounds, move(bounds, target)])
    flips = np.array([[[k1 * 4 + k0 * 2 + dx for k0 in (0, 1)] for k1 in (0, 1)] for dx in (0, 1)])
    blocks = jnp.bitwise_xor(exp, jnp.asarray(flips, jnp.int32))
    position = blocks[..., None] * tok_count + jnp.arange(tok_count, dtype=jnp.int32)
    position = position[None, None, ..., None, :]

    def spread(side):
        return bounds[:, :, side][:, :, None, None, None, :, None]

    return weights, ((position >= spread(0)) & (position < spread(1))).astype(jnp.float32)


def hold_kernel(*refs):
    count = (len(refs) - 1) // 2
    copies = [
        pltpu.make_async_copy(refs[at], refs[count + at], refs[-1].at[at]) for at in range(count)
    ]
    for copy in copies:
        copy.start()
    for copy in copies:
        copy.wait()


def hold(*arrays):
    return pl.pallas_call(
        hold_kernel,
        out_shape=[pltpu.VMEM(array.shape, array.dtype) for array in arrays],
        in_specs=[pl.BlockSpec(memory_space=pltpu.HBM)] * len(arrays),
        out_specs=[pl.BlockSpec(memory_space=pltpu.VMEM)] * len(arrays),
        scratch_shapes=[pltpu.SemaphoreType.DMA((len(arrays),))],
        compiler_params=pltpu.CompilerParams(vmem_limit_bytes=1024 * 1024),
        cost_estimate=pl.CostEstimate(
            flops=0, bytes_accessed=4 * sum(array.size for array in arrays), transcendentals=0
        ),
        name="hold_weights",
    )(*[pltpu.with_memory_space_constraint(array, pltpu.HBM) for array in arrays])


def assemble_kernel(plan, *refs):
    flag_ref, refs = refs[0], refs[1:]
    outs = refs[sum(len(places) for pieces in plan for _, _, places in pieces) :]
    at = 0
    for out_ref, pieces in zip(outs, plan):
        first = 0
        for size, pick, places in pieces:
            held = [refs[at + index][...] for index in range(len(places))]
            at += len(places)
            if pick:
                value = jnp.where(flag_ref[0] == 1, held[0], held[1])
            else:
                value = held[0]
                if len(held) > 1:
                    value = value.astype(jnp.float32)
                    for term in held[1:]:
                        value = value + term.astype(jnp.float32)
            out_ref[first : first + size] = value.astype(out_ref.dtype)
            first += size


def assemble(flag, *outputs, steps=2):
    width = outputs[0][0][2][0][0].shape[1]
    wide = width // steps
    operands, specs = [], []

    def block(row):
        return lambda j: (row, j)

    for pieces in outputs:
        for size, _, terms in pieces:
            for array, first in terms:
                operands.append(array)
                specs.append(pl.BlockSpec((size, wide), block(first // size)))
    rows = [sum(size for size, _, _ in pieces) for pieces in outputs]
    return pl.pallas_call(
        functools.partial(assemble_kernel, outputs_plan(outputs)),
        grid=(steps,),
        out_shape=[jax.ShapeDtypeStruct((count, width), jnp.bfloat16) for count in rows],
        in_specs=[pl.BlockSpec(memory_space=pltpu.SMEM)] + specs,
        out_specs=[pl.BlockSpec((count, wide), lambda j: (0, j)) for count in rows],
        compiler_params=pltpu.CompilerParams(vmem_limit_bytes=16 * 1024 * 1024),
        cost_estimate=pl.CostEstimate(
            flops=2 * sum(rows) * width, bytes_accessed=8 * sum(rows) * width, transcendentals=0
        ),
        name="assemble",
    )(flag, *operands)


def outputs_plan(outputs):
    return [[(size, pick, [None] * len(terms)) for size, pick, terms in out] for out in outputs]


def experts_dense(resid, normed, weights, member, gate_weight, up_weight, down_weight, score_weight):
    f32 = jnp.float32
    n = normed.shape[0]
    h = n // 2
    z = lax.axis_index("exp") // GRID[0]
    middle = ((z == 1) | (z == 2)).astype(jnp.int32)[None]
    rest = jnp.dot(down_weight[0].astype(f32), score_weight, precision=lax.Precision.HIGHEST)
    terms = []
    for _ in range(3):
        terms.append(rest.astype(jnp.bfloat16))
        rest = rest - terms[-1].astype(f32)
    relevance = jnp.pad(jnp.stack(terms), ((0, 13), (0, 0)))
    calls = {
        "0": [(0, i) for i in range(4)],
        "p": [(1, i) for i in range(3)],
        "q": [(2, i) for i in range(3)],
        "r": [(3, i) for i in range(3)],
        "e": [(3, 3), (2, 3), (1, 3)],
    }
    order = [
        (name, slot, side, i)
        for name, blocks in calls.items()
        for side in (1, 0)
        for slot, i in blocks
    ]
    own_score = jnp.dot(resid.astype(f32), score_weight, precision=lax.Precision.HIGHEST)
    by_slot = weights.transpose(3, 4, 0, 1, 2, 5).reshape(4, 2, 4, n)
    scale = jnp.stack([by_slot[slot, side, i] for _, slot, side, i in order])
    own_sums = jnp.sum(member[0, 0, 0, 0, 0] * own_score[None], axis=1)
    experts = (gate_weight, up_weight, down_weight)
    normed, scale, member, relevance = together(normed, scale, member, relevance)

    def join(*blocks):
        return jnp.concatenate(blocks, axis=0)

    def work(held, name, *rows, side=1):
        first = [entry[0] for entry in order].index(name) + (1 - side) * len(calls[name])
        return weighted_pieces(rows, scale, first, relevance, held or experts, bool(held))

    def swap(rows):
        return move(rows, over_core)

    def keep(size, array, first=0):
        return (size, False, [(array, first)])

    p, m = move(normed, z_pair), move(normed, z_middle)
    x0, y0 = move(normed, over_x), move(normed, over_y)
    p, m, x0, y0, experts = together(p, m, x0, y0, experts)
    held = hold(*experts)

    to_x, to_y = assemble(
        middle, [keep(n, p), keep(h, y0, h)], [keep(n, p), keep(h, x0)], steps=1
    )
    px, py = move(to_x, over_x), move(to_y, over_y)
    q_middle, q_end = move(p, z_middle), move(m, z_outward)
    px, py, q_middle, q_end, held = together(px, py, q_middle, q_end, held)

    (q,) = assemble(middle, [(n, True, [(q_middle, 0), (q_end, 0)])], steps=1)
    qx, qy = move(q, over_x), move(q, over_y)
    r_end = move(q, z_outward)
    d0 = join(py[n:], px[n:])
    rows_0 = join(normed, x0, y0, d0)
    out_0 = work(held, "0", swap(rows_0), rows_0)
    qx, qy, r_end, out_0 = together(qx, qy, r_end, out_0)

    pick = (n, True, [(m, 0), (r_end, 0)])
    to_x, to_y, r = assemble(
        middle, [pick, keep(h, qy, h)], [pick, keep(h, qx)], [pick], steps=1
    )
    rx, ry = move(to_x, over_x), move(to_y, over_y)
    dp = move(d0, z_pair)
    rows_p = join(p, px[:n], py[:n])
    rows_q = join(q, qx, qy)
    other_q = swap(rows_q)
    out_p = work(held, "p", swap(rows_p), rows_p)
    out_q = work(held, "q", other_q, rows_q)
    rx, ry, dp, out_p, out_q = together(rx, ry, dp, out_p, out_q)

    by_x, by_y = move(ry[h:n], over_x), move(rx[:h], over_y)
    rows_r = join(r, rx[:n], ry[:n])
    other_r, came_p = swap(rows_r), swap(out_p[0])
    mine_r = work(held, "r", rows_r, side=0)
    by_x, by_y, other_r, mine_r, came_p, out_0, out_q = together(
        by_x, by_y, other_r, mine_r, came_p, out_0, out_q
    )

    rows_e = join(by_y, by_x, ry[n:], rx[n:], dp)
    other_e = swap(rows_e)
    def far(array):
        return pltpu.with_memory_space_constraint(array, pltpu.HBM)

    def both(size, out, came, first, *more):
        return (size, False, [(far(out[1]), first), (far(came), first), *more])

    def of_x(out, came, more):
        return [both(h, out, came, n, more), both(h, out, came, n + h)]

    def of_y(out, came, more):
        return [both(h, out, came, 2 * n), both(h, out, came, 2 * n + h, more)]

    def own(out, came, *more):
        return [both(n, out, came, 0, *[(array, 0) for array in more])]

    to_x, to_y = assemble(middle, [both(n, out_p, came_p, n)], [both(n, out_p, came_p, 2 * n)])
    px, py = move(to_x, over_x), move(to_y, over_y)
    came_0 = swap(out_0[0])
    out_e = work(held, "e", other_e, rows_e)
    came_e = swap(out_e[0])
    other_r, out_e, px, py = together(other_r, out_e, px, py)
    theirs_r = work(held, "r", other_r, side=1)
    out_r = (theirs_r[0], mine_r[0], jnp.concatenate([theirs_r[1], mine_r[1]], axis=0))
    came_r = swap(theirs_r[0])
    to_y, to_x = assemble(middle, [both(h, out_e, came_e, 0)], [both(h, out_e, came_e, h)])
    from_y, from_x = move(to_y, over_y), move(to_x, over_x)
    outs = {"0": out_0, "p": out_p, "q": out_q, "r": out_r, "e": out_e}
    rows = join(*[outs[name][2] for name in calls])
    from_y, from_x, came_0, came_r, out_q, rows = together(
        from_y, from_x, came_0, came_r, out_q, rows
    )
    found = {(slot, side, i): at for at, (_, slot, side, i) in enumerate(order)}
    scores = jnp.stack(
        [rows[found[slot, side, i]] for side in (0, 1) for i in range(4) for slot in range(4)]
    ).reshape(2, 2, 2, 2, 2, n)
    doc_sums = jnp.sum(member * scores[..., None, :], axis=(2, 3, 4, 6))
    doc_sums = doc_sums.at[0, 0].add(own_sums)
    req = lax.axis_index("req")
    doc_sums = jnp.where(req % 2 == 1, doc_sums[::-1], doc_sums)
    doc_sums = jnp.where(req // 2 == 1, doc_sums[:, ::-1], doc_sums)
    doc_sums = jnp.broadcast_to(
        doc_sums.transpose(1, 0, 2)[:, :, None], (2, 2, lax.axis_size("exp"), doc_sums.shape[2])
    ).reshape(-1, doc_sums.shape[2])
    to_x, to_y, to_pair = assemble(
        middle,
        of_x(out_r, came_r, (from_y, 0)) + [both(h, out_e, came_e, n + h)],
        of_y(out_r, came_r, (from_x, 0)) + [both(h, out_e, came_e, n)],
        [both(n, out_e, came_e, 2 * n)],
    )
    rx, ry = move(to_x, over_x), move(to_y, over_y)
    d_more = move(to_pair, z_pair)
    came_q = swap(out_q[0])
    doc_sums = lax.all_to_all(doc_sums, ALL, split_axis=0, concat_axis=0, tiled=True)
    rx, ry, d_more, doc_sums, came_q = together(rx, ry, d_more, doc_sums, came_q)

    to_x, to_y, sum_r = assemble(
        middle,
        of_x(out_q, came_q, (ry, n)),
        of_y(out_q, came_q, (rx, n)),
        own(out_r, came_r, rx, ry),
    )
    qx, qy = move(to_x, over_x), move(to_y, over_y)
    q_more = move(sum_r, z_inward)
    qx, qy, q_more = together(qx, qy, q_more)

    to_x, to_y, sum_q = assemble(
        middle,
        [both(h, out_0, came_0, 3 * n + h, (d_more, h))],
        [both(h, out_0, came_0, 3 * n, (d_more, 0))],
        own(out_q, came_q, qx, qy, q_more),
    )
    d_x, d_y = move(to_x, over_x), move(to_y, over_y)
    p_more, r_more = move(sum_q, z_middle), move(sum_q, z_inward)
    d_x, d_y, p_more, r_more = together(d_x, d_y, p_more, r_more)

    to_x, to_y, sum_p, sum_r = assemble(
        middle,
        of_x(out_0, came_0, (d_y, 0)),
        of_y(out_0, came_0, (d_x, 0)),
        own(out_p, came_p, px, py, p_more),
        own(out_r, came_r, rx, ry, r_more),
    )
    x0, y0 = move(to_x, over_x), move(to_y, over_y)
    from_p, from_r = move(sum_p, z_pair), move(sum_r, z_middle)
    (layer_out,) = assemble(middle, own(out_0, came_0, x0, y0, from_p, from_r, resid))
    return layer_out, jnp.sum(doc_sums, axis=0)


def is_small():
    return (lax.axis_size("req"), lax.axis_size("exp")) == (2 * GRID[1], GRID[0] * GRID[2])


def local(
    hidden_in,
    qkv,
    q_gain,
    k_gain,
    query_pages,
    page_table,
    doc_lengths,
    doc_query,
    out_weight,
    moe_gain,
    routes,
    route_weight,
    gate_weight,
    up_weight,
    down_weight,
    score_weight,
):
    tok_count = hidden_in.shape[0]
    exp_index = lax.axis_index("exp")
    doc_len = doc_lengths[0]
    tables = start_tables(routes, route_weight) if is_small() else doc_len
    attn, tables = attention(
        qkv, q_gain, k_gain, query_pages, page_table, doc_lengths, doc_query, tables
    )
    attn = attn.transpose(1, 0, 2).reshape(hidden_in.shape)
    mixed = jnp.dot(attn, out_weight, preferred_element_type=jnp.float32)
    resid = (hidden_in.astype(jnp.float32) + mixed).astype(jnp.bfloat16)
    normed = rms_scale(resid.astype(jnp.float32), moe_gain).astype(jnp.bfloat16)
    if is_small():
        weights, member = finish_tables(tables, doc_len)
        layer_out, doc_sums = experts_dense(
            resid,
            normed,
            weights,
            member,
            gate_weight,
            up_weight,
            down_weight,
            score_weight,
        )
        return (layer_out, (doc_sums / doc_len.astype(jnp.float32))[None, :])
    combined = experts_by_slots(
        normed, routes, route_weight, gate_weight, up_weight, down_weight
    )
    layer_out = (resid.astype(jnp.float32) + combined).astype(jnp.bfloat16)
    token_score = jnp.dot(
        layer_out.astype(jnp.float32), score_weight, precision=lax.Precision.HIGHEST
    )
    doc_ends = jnp.cumsum(doc_len, dtype=jnp.int32)
    own_pos = exp_index * tok_count + jnp.arange(tok_count, dtype=jnp.int32)
    member = (own_pos[:, None] < doc_ends[None, :]) & (
        own_pos[:, None] >= (doc_ends - doc_len)[None, :]
    )
    doc_partial = jnp.dot(
        token_score, member.astype(jnp.float32), precision=lax.Precision.HIGHEST
    )
    doc_sums = lax.psum(doc_partial, "exp")
    doc_scores = (doc_sums / doc_len.astype(jnp.float32))[None, :]
    return (layer_out, doc_scores)


def solution(mesh):
    in_specs = (
        P(("req", "exp"), None),
        P(("req", "exp"), None),
        P(),
        P(),
        P("req", None, None, "exp"),
        P("req", None),
        P("req", None),
        P("req", None),
        P(),
        P(),
        P(("req", "exp"), None),
        P(("req", "exp"), None),
        P(("req", "exp"), None, None),
        P(("req", "exp"), None, None),
        P(("req", "exp"), None, None),
        P(),
    )
    out_specs = (P(("req", "exp"), None), P("req", None))
    return jax.shard_map(local, mesh=mesh, in_specs=in_specs, out_specs=out_specs, check_vma=False)
```
